32 devices in a mesh: dp: 8 (over y, x, core), tensor: 4 (over z).
Axes of the slice: x: 2, y: 2, z: 4, core: 2. Of those that a mesh axis runs over, the one named last changes fastest.
Arguments:
- tokens: bfloat16 [8192, 2048], P(('dp', 'tensor')), may hold values from -6 to 6
- seq_lengths: int32 [8, 2], P('dp'), may hold values from 1 to 768, 1024 in all within a row
- attn_gain: float32 [2048], replicated, may hold values from 0.1 to 1.9
- mlp_gain: float32 [2048], replicated, may hold values from 0.1 to 1.9
- q_gain: float32 [128], replicated, may hold values from 0.1 to 1.9
- k_gain: float32 [128], replicated, may hold values from 0.1 to 1.9
- w_query: bfloat16 [2048, 2048], P(None, 'tensor'), may hold values from -0.125 to 0.125
- key_weight: bfloat16 [2048, 1024], P(None, 'tensor'), may hold values from -0.125 to 0.125
- value_weight: bfloat16 [2048, 1024], P(None, 'tensor'), may hold values from -0.125 to 0.125
- w_out: bfloat16 [2048, 2048], P('tensor'), may hold values from -0.5 to 0.5
- w_gate: bfloat16 [2048, 6144], P(None, 'tensor'), may hold values from -0.125 to 0.125
- w_up: bfloat16 [2048, 6144], P(None, 'tensor'), may hold values from -0.125 to 0.125
- w_down: bfloat16 [6144, 2048], P('tensor'), may hold values from -0.078125 to 0.078125
- out_grad: bfloat16 [8192, 2048], P(('dp', 'tensor')), may hold values from -6 to 6
Outputs:
- output: bfloat16 [8192, 2048], P(('dp', 'tensor'))
- token_grad: bfloat16 [8192, 2048], P(('dp', 'tensor'))
- attn_gain_grad: float32 [2048], replicated
- mlp_gain_grad: float32 [2048], replicated
- q_gain_grad: float32 [128], replicated
- k_gain_grad: float32 [128], replicated
- w_query_grad: float32 [2048, 2048], P('dp', 'tensor')
- w_key_grad: float32 [2048, 1024], P('dp', 'tensor')
- w_value_grad: float32 [2048, 1024], P('dp', 'tensor')
- w_out_grad: float32 [2048, 2048], P('tensor', 'dp')
- w_gate_grad: float32 [2048, 6144], P('dp', 'tensor')
- w_up_grad: float32 [2048, 6144], P('dp', 'tensor')
- w_down_grad: float32 [6144, 2048], P('tensor', 'dp')
The draws below stay inside these ranges and needn't reach their ends.
Inputs may be any that keep to these rules, and one draw needn't show every extreme that they name: `seq_lengths`: row d lists in order the lengths of the 2 sequences packed one after another into the 1024 tokens of index d of dp; each row sums to 1024 and its longest is at most 768.
All inputs are finite; a program needn't handle non-finite values.
Results may differ from the reference program's by a relative error of at most 0.02.
Values may be sent and summed in bfloat16 or wider, within the bound.
No kernel may reach another device: no remote copies, remote signals or barrier semaphores. Data moves between devices by JAX's collectives and lax.ppermute only.
A program may use at most 192 MiB of HBM per device.

```python
import math
import jax
import jax.numpy as jnp
import numpy as np
from jax import lax

MODEL_DIM = 2048
QUERY_HEAD_COUNT = 16
KEY_VALUE_HEADS = 8
HEAD_SIZE = 128
FF = 6144
TOK_DEV = 1024
SEQ_DEV = 2
LONGEST = 768
TOKENS = 8192
N_DP = 8


def raised(entries, own_key, source, target, shards_of, factor):
    owner, partner = [(jnp.arange(entries.shape[axis_at]) // (entries.shape[axis_at] // shards_of)).reshape([-1 if axis == axis_at else 1 for axis in range(entries.ndim)]) for axis_at in (source, target)]
    chosen = jax.random.permutation(own_key, shards_of)[partner]
    strong = (owner == chosen) | (owner == (partner + shards_of // 2) % shards_of)
    return jnp.where(strong, factor * entries, entries)


def level_of(key, dims, cuts, smallest, largest):
    gain = 1.0
    for axis_at, blocks in cuts:
        draws = jax.random.uniform(jax.random.fold_in(jax.random.fold_in(key, 6), axis_at), (blocks,), jnp.float32, smallest / len(cuts), largest / len(cuts))
        gain = gain * jnp.repeat(jnp.exp(draws), dims[axis_at] // blocks).reshape((-1,) + (1,) * (len(dims) - 1 - axis_at))
    return gain


def profile(amount, total, reach, lean):
    portions = [(1 << 20) // math.isqrt(rank ** lean) + 1 for rank in range(2, amount + 1)]
    surplus, counts = total - reach - (amount - 1), [1] * (amount - 1)
    while surplus > 0:
        movable = [i for i in range(amount - 1) if counts[i] < reach]
        pool, left = sum([portions[i] for i in movable]), surplus
        for i in movable:
            addition = min(reach - counts[i], max(1, left * portions[i] // pool), surplus)
            counts[i] = counts[i] + addition
            surplus = surplus - addition
    return np.array([reach] + counts)


def ragged(key, number_of, total, limit, lean):
    if number_of == 2:
        one = jax.random.randint(key, (), max(1, total - limit), min(limit, total - 1) + 1)
        return jnp.stack([one, total - one])
    sizes = jnp.asarray(profile(number_of, total, limit, lean), jnp.int32)
    pairs = (number_of - 1) // 2
    giver, sink = sizes[1:1 + 2 * pairs:2], sizes[2:2 + 2 * pairs:2]
    room = jnp.minimum(giver - 1, limit - sink)
    moved = jax.random.randint(jax.random.fold_in(key, 1), (pairs,), 0, 1 << 20) % (room + 1)
    sizes = sizes.at[1:1 + 2 * pairs:2].set(giver - moved).at[2:2 + 2 * pairs:2].set(sink + moved)
    return sizes[jax.random.permutation(jax.random.fold_in(key, 2), number_of)]


def bell_draw(own_key, extent, scale, reach, pieces=(), kind=jnp.bfloat16):
    factor_of = level_of(own_key, extent, pieces, -0.22, 0.18) if pieces else 1.0
    drawn = jax.random.normal(own_key, extent, jnp.float32) * scale * factor_of
    return jnp.minimum(jnp.maximum(drawn, -reach), reach).astype(kind)


def gaussian_with(own_key, shape, scale, reach, cuts, heavy, kind=jnp.bfloat16):
    values = scale * jax.random.normal(own_key, shape, jnp.float32)
    if cuts:
        values = values * level_of(own_key, shape, cuts, -0.22, 0.18)
    return jnp.clip(raised(values, jax.random.fold_in(own_key, 3), *heavy), -reach, reach).astype(kind)


def setup_inputs(seed: int = 0) -> dict:
    splits = jax.random.split(jax.random.key(seed), 15)
    return {
        "tokens": bell_draw(splits[0], (TOKENS, MODEL_DIM), 1.0, 6.0, ((0, 32),)),
        "seq_lengths": jax.vmap(lambda own: ragged(own, SEQ_DEV, TOK_DEV, LONGEST, 2))(jax.random.split(splits[1], N_DP)).reshape((N_DP, SEQ_DEV)).astype(jnp.int32),
        "attn_gain": jnp.clip(1.0 + 0.18 * jax.random.normal(splits[2], (MODEL_DIM,), jnp.float32), 0.1, 1.9),
        "mlp_gain": jnp.clip(1.0 + 0.18 * jax.random.normal(splits[3], (MODEL_DIM,), jnp.float32), 0.1, 1.9),
        "q_gain": jnp.clip(1.0 + 0.18 * jax.random.normal(splits[4], (HEAD_SIZE,), jnp.float32), 0.1, 1.9),
        "k_gain": jnp.clip(1.0 + 0.18 * jax.random.normal(splits[5], (HEAD_SIZE,), jnp.float32), 0.1, 1.9),
        "w_query": bell_draw(splits[6], (MODEL_DIM, QUERY_HEAD_COUNT * HEAD_SIZE), MODEL_DIM ** -0.5, 0.125, ((1, 4),)),
        "key_weight": bell_draw(splits[7], (MODEL_DIM, KEY_VALUE_HEADS * HEAD_SIZE), MODEL_DIM ** -0.5, 0.125, ((1, 4),)),
        "value_weight": bell_draw(splits[8], (MODEL_DIM, KEY_VALUE_HEADS * HEAD_SIZE), MODEL_DIM ** -0.5, 0.125, ((1, 4),)),
        "w_out": bell_draw(splits[9], (QUERY_HEAD_COUNT * HEAD_SIZE, MODEL_DIM), (QUERY_HEAD_COUNT * HEAD_SIZE // 16) ** -0.5, 0.5, ((0, 4),)),
        "w_gate": bell_draw(splits[10], (MODEL_DIM, FF), MODEL_DIM ** -0.5, 0.125, ((1, 4),)),
        "w_up": bell_draw(splits[11], (MODEL_DIM, FF), MODEL_DIM ** -0.5, 0.125, ((1, 4),)),
        "w_down": bell_draw(splits[12], (FF, MODEL_DIM), FF ** -0.5, 0.078125, ((0, 4),)),
        "out_grad": gaussian_with(splits[13], (TOKENS, MODEL_DIM), 1.0, 6.0, ((0, 32),), (0, 1, 32, 2.75)),
    }


NORM_EPSILON = 1e-06
ROPE_BASE = 1000000.0
MASK_FILL = -1e+30
HIGHEST_PRECISION = lax.Precision.HIGHEST

@jax.custom_vjp
def reduced_precision(v):
    return lax.optimization_barrier(v.astype(jnp.bfloat16)).astype(jnp.float32)

@jax.custom_vjp
def reduced_precision_back(v):
    return v

def low_keep(v):
    return (reduced_precision(v), None)

def low_pass(kept, grad):
    return (grad,)

def back_keep(v):
    return (v, None)

def back_low(kept, grad):
    return (reduced_precision(grad),)
reduced_precision.defvjp(low_keep, low_pass)
reduced_precision_back.defvjp(back_keep, back_low)

def normed(values):
    return values * lax.rsqrt(lax.optimization_barrier(jnp.mean(values * values, axis=-1, keepdims=True)) + NORM_EPSILON)

def matrix_multiply(first_operand, second_operand):
    return jnp.dot(first_operand, second_operand, precision=HIGHEST_PRECISION, preferred_element_type=jnp.float32)

def positions_of(lengths, count_of_rows):
    seq_ends = jnp.cumsum(lengths, dtype=jnp.int32)
    starts = seq_ends - lengths
    place_index = jnp.arange(count_of_rows, dtype=jnp.int32)
    segment = lax.optimization_barrier(jnp.sum((place_index[:, None] >= seq_ends[None, :]).astype(jnp.int32), axis=1, dtype=jnp.int32))
    belongs = segment[:, None] == jnp.arange(lengths.shape[0], dtype=jnp.int32)[None, :]
    offset = lax.optimization_barrier(jnp.sum(jnp.where(belongs, starts[None, :], 0), axis=1, dtype=jnp.int32))
    return (segment, place_index - offset)

def rope_tables(position, head_width):
    half_width = head_width // 2
    frequency = ROPE_BASE ** (-2.0 * jnp.arange(half_width, dtype=jnp.float32) / head_width)
    angles = position.astype(jnp.float32)[:, None] * frequency[None, :]
    cosine_table = jnp.concatenate([jnp.cos(angles), jnp.cos(angles)], axis=1)
    sine_table = jnp.concatenate([jnp.sin(angles), jnp.sin(angles)], axis=1)
    return (cosine_table[:, None, :], sine_table[:, None, :])

def rotate(values):
    half_width = values.shape[-1] // 2
    return jnp.concatenate([-values[..., half_width:], values[..., :half_width]], axis=-1)

def apply_rope(values, cosine_table, sine_table):
    return values * cosine_table + rotate(values) * sine_table

def attention(query_operand, key_side, value_operand, segment):
    count_of_rows = query_operand.shape[0]
    group_width = QUERY_HEAD_COUNT // KEY_VALUE_HEADS
    tile_rows = min(512, count_of_rows)
    grouped_heads = query_operand.reshape(count_of_rows, KEY_VALUE_HEADS, group_width, HEAD_SIZE)
    columns = jnp.arange(count_of_rows, dtype=jnp.int32)

    def one_tile(number):
        first_row = (number * tile_rows).astype(jnp.int32)
        query_rows = lax.dynamic_slice_in_dim(grouped_heads, first_row, tile_rows, 0)
        row_segment = lax.dynamic_slice_in_dim(segment, first_row, tile_rows, 0)
        row_place = first_row + jnp.arange(tile_rows, dtype=jnp.int32)
        visible = (row_segment[:, None] == segment[None, :]) & (row_place[:, None] >= columns[None, :])
        scores = reduced_precision_back(jnp.einsum('qhgd,shd->hgqs', query_rows, key_side, precision=HIGHEST_PRECISION))
        scores = jnp.where(visible, scores, MASK_FILL)
        row_peak = lax.optimization_barrier(jnp.max(scores, axis=-1, keepdims=True))
        spread = jnp.exp(scores - row_peak)
        soft_weights = reduced_precision(spread / lax.optimization_barrier(jnp.sum(spread, axis=-1, keepdims=True)))
        return jnp.einsum('hgqs,shd->qhgd', soft_weights, value_operand, precision=HIGHEST_PRECISION)
    mixed_tiles = lax.map(jax.checkpoint(one_tile), jnp.arange(count_of_rows // tile_rows, dtype=jnp.int32))
    return mixed_tiles.reshape(count_of_rows, QUERY_HEAD_COUNT * HEAD_SIZE)

def layer_block(values, segment, position, weights):
    attn_gain, mlp_gain, q_gain, k_gain, w_query, key_weight, value_weight, w_out, w_gate, w_up, w_down = weights
    count_of_rows = values.shape[0]
    attention_start = reduced_precision(normed(values) * attn_gain)
    query_raw = reduced_precision_back(matrix_multiply(attention_start, w_query)).reshape(count_of_rows, QUERY_HEAD_COUNT, HEAD_SIZE)
    key_unnormed = reduced_precision_back(matrix_multiply(attention_start, key_weight)).reshape(count_of_rows, KEY_VALUE_HEADS, HEAD_SIZE)
    value_operand = reduced_precision(reduced_precision_back(matrix_multiply(attention_start, value_weight))).reshape(count_of_rows, KEY_VALUE_HEADS, HEAD_SIZE)
    cosine_table, sine_table = rope_tables(position, HEAD_SIZE)
    query_operand = reduced_precision(apply_rope(normed(query_raw) * q_gain, cosine_table, sine_table) * HEAD_SIZE ** (-0.5))
    key_side = reduced_precision(apply_rope(normed(key_unnormed) * k_gain, cosine_table, sine_table))
    attn_mixed = reduced_precision(reduced_precision_back(attention(query_operand, key_side, value_operand, segment)))
    hidden = values + reduced_precision_back(matrix_multiply(attn_mixed, w_out))
    mlp_entry = reduced_precision(normed(hidden) * mlp_gain)
    gate_proj = reduced_precision_back(matrix_multiply(mlp_entry, w_gate))
    up_proj = reduced_precision_back(matrix_multiply(mlp_entry, w_up))
    active = reduced_precision(gate_proj * jax.nn.sigmoid(gate_proj) * up_proj)
    return hidden + matrix_multiply(active, w_down)

def reference(tokens, seq_lengths, attn_gain, mlp_gain, q_gain, k_gain, w_query, key_weight, value_weight, w_out, w_gate, w_up, w_down, out_grad):
    model_width = tokens.shape[1]
    inputs = tokens.astype(jnp.float32).reshape(N_DP, TOK_DEV, model_width)
    segments, positions = jax.vmap(lambda lengths: positions_of(lengths, TOK_DEV))(seq_lengths)
    params = (attn_gain.astype(jnp.float32), mlp_gain.astype(jnp.float32), q_gain.astype(jnp.float32), k_gain.astype(jnp.float32), w_query.astype(jnp.float32), key_weight.astype(jnp.float32), value_weight.astype(jnp.float32), w_out.astype(jnp.float32), w_gate.astype(jnp.float32), w_up.astype(jnp.float32), w_down.astype(jnp.float32))

    def forward(values, weights):

        def block_step(unused_carry, block_data):
            block_values, segment, position = block_data
            return (unused_carry, layer_block(block_values, segment, position, weights))
        unused_final, result = lax.scan(block_step, None, (values, segments, positions))
        return result
    result, pullback = jax.vjp(forward, inputs, params)
    input_grad, weight_grads = pullback(out_grad.astype(jnp.float32).reshape(N_DP, TOK_DEV, model_width))
    return (result.reshape(N_DP * TOK_DEV, model_width).astype(jnp.bfloat16), input_grad.reshape(N_DP * TOK_DEV, model_width).astype(jnp.bfloat16), weight_grads[0], weight_grads[1], weight_grads[2], weight_grads[3], weight_grads[4], weight_grads[5], weight_grads[6], weight_grads[7], weight_grads[8], weight_grads[9], weight_grads[10])
```

```python
import functools

import jax
import jax.numpy as jnp
from jax import lax
from jax.experimental import pallas as pl
from jax.experimental.pallas import tpu as pltpu
from jax.sharding import PartitionSpec as P

NORM_EPSILON = 1e-06
ROPE_BASE = 1000000.0
MASK_FILL = -1e30
VMEM_BYTES = 52 * 1024 * 1024
F32 = jnp.float32
BF16 = jnp.bfloat16

NT = (((1,), (1,)), ((), ()))
TN = (((0,), (0,)), ((), ()))


def mm(a, b):
    return jnp.dot(a, b, preferred_element_type=F32)


def mm_nt(a, b):
    return lax.dot_general(a, b, NT, preferred_element_type=F32)


def mm_tn(a, b):
    return lax.dot_general(a, b, TN, preferred_element_type=F32)


def inv_root_of(values):
    return lax.rsqrt(jnp.mean(values * values, axis=-1, keepdims=True) + NORM_EPSILON)


def norm_back(grad_normed, normal, inv_root):
    return inv_root * (
        grad_normed - normal * jnp.mean(grad_normed * normal, axis=-1, keepdims=True)
    )


def call(kernel, grid_spec, out_shape, flops, nbytes, aliases=None):
    return pl.pallas_call(
        kernel,
        grid_spec=grid_spec,
        out_shape=out_shape,
        input_output_aliases=aliases or {},
        compiler_params=pltpu.CompilerParams(vmem_limit_bytes=VMEM_BYTES),
        cost_estimate=pl.CostEstimate(flops=flops, bytes_accessed=nbytes, transcendentals=0),
    )


def shape(dims, dtype):
    return jax.ShapeDtypeStruct(dims, dtype)


def positions_of(lengths, count_of_rows):
    seq_ends = jnp.cumsum(lengths, dtype=jnp.int32)
    starts = seq_ends - lengths
    place_index = jnp.arange(count_of_rows, dtype=jnp.int32)
    segment = jnp.sum(
        (place_index[:, None] >= seq_ends[None, :]).astype(jnp.int32), axis=1, dtype=jnp.int32
    )
    belongs = segment[:, None] == jnp.arange(lengths.shape[0], dtype=jnp.int32)[None, :]
    offset = jnp.sum(jnp.where(belongs, starts[None, :], 0), axis=1, dtype=jnp.int32)
    return (offset, place_index - offset)


def rope_tables(position, head_width):
    half_width = head_width // 2
    frequency = ROPE_BASE ** (-2.0 * jnp.arange(half_width, dtype=F32) / head_width)
    angles = position.astype(F32)[:, None] * frequency[None, :]
    cosine, sine = jnp.cos(angles), jnp.sin(angles)
    return (
        jnp.concatenate([cosine, cosine], axis=1),
        jnp.concatenate([-sine, sine], axis=1),
    )


def qkv_kernel(heads, kv_heads, dim, sid_ref, x_ref, gain_ref, w_ref, cos_ref, sin_ref, qg_ref, kg_ref, *refs):
    entry_ref, side_ref, raw_ref = refs[-3:]
    x = x_ref[...].astype(F32)
    entry = (x * inv_root_of(x) * gain_ref[...]).astype(BF16)
    entry_ref[...] = entry
    both = mm(entry, w_ref[...])
    cosine, sine = cos_ref[...], sin_ref[...]
    for h in range(heads + kv_heads):
        cols = slice(h * dim, (h + 1) * dim)
        raw = both[:, cols]
        raw_ref[:, cols] = raw.astype(BF16)
        gain = qg_ref[...] if h < heads else kg_ref[...]
        u = raw * inv_root_of(raw) * gain
        turned = u * cosine + pltpu.roll(u, dim // 2, 1) * sine
        if h < heads:
            turned = turned * dim ** (-0.5)
        side_ref[:, cols] = turned.astype(BF16)
    rest = slice((heads + kv_heads) * dim, (heads + 2 * kv_heads) * dim)
    side_ref[:, rest] = both[:, rest].astype(BF16)


def qkv_shard(sid, x, gain, w_qkv, cosine, sine, q_gain, k_gain, heads, kv_heads, dim, block_rows, kept):
    rows, width = x.shape
    cols = w_qkv.shape[1]
    raw_cols = (heads + kv_heads) * dim
    whole = lambda i, sid: (0, 0)
    mine = lambda i, sid: (sid[0], 0)
    in_specs = [
        pl.BlockSpec((rows, width), whole),
        pl.BlockSpec((1, width), whole),
        pl.BlockSpec((width, cols), whole),
        pl.BlockSpec((rows, dim), mine),
        pl.BlockSpec((rows, dim), mine),
        pl.BlockSpec((1, dim), whole),
        pl.BlockSpec((1, dim), whole),
    ]
    args = [sid, x, gain, w_qkv, cosine, sine, q_gain, k_gain]
    aliases = {}
    if kept is not None:
        for j, array in enumerate(kept):
            aliases[len(args)] = j
            args.append(array)
            in_specs.append(pl.BlockSpec(memory_space=pl.ANY))
    return call(
        functools.partial(qkv_kernel, heads, kv_heads, dim),
        pltpu.PrefetchScalarGridSpec(
            num_scalar_prefetch=1,
            grid=(1,),
            in_specs=in_specs,
            out_specs=[
                pl.BlockSpec((rows, width), mine),
                pl.BlockSpec((rows, cols), mine),
                pl.BlockSpec((rows, raw_cols), mine),
            ],
        ),
        [
            shape((block_rows, width), BF16),
            shape((block_rows, cols), BF16),
            shape((block_rows, raw_cols), BF16),
        ],
        2 * rows * width * cols,
        2 * (2 * rows * width + width * cols + 2 * rows * cols),
        aliases,
    )(*args)


def visible_keys(start_ref, first_row, rows, keys):
    row = first_row + lax.broadcasted_iota(jnp.int32, (rows, keys), 0)
    col = lax.broadcasted_iota(jnp.int32, (rows, keys), 1)
    return (col <= row) & (col >= start_ref[first_row : first_row + rows, :])


def attention_kernel(n, heads, kv_heads, dim, z_ref, side_ref, start_ref, mixed_ref, lse_ref):
    rows = side_ref.shape[0] // n
    group = heads // kv_heads
    for i in range(n):
        slot = lax.rem(i - z_ref[0] + n, n)
        keys = (i + 1) * rows
        here = slice(i * rows, (i + 1) * rows)
        visible = visible_keys(start_ref, i * rows, rows, keys)
        for h in range(heads):
            kv = h // group
            key = side_ref[:keys, (heads + kv) * dim : (heads + kv + 1) * dim]
            value = side_ref[
                :keys, (heads + kv_heads + kv) * dim : (heads + kv_heads + kv + 1) * dim
            ]
            cols = slice(h * dim, (h + 1) * dim)
            scores = jnp.where(visible, mm_nt(side_ref[here, cols], key), MASK_FILL)
            peak = jnp.max(scores, axis=-1, keepdims=True)
            spread = jnp.exp(scores - peak)
            total = jnp.sum(spread, axis=-1, keepdims=True)
            mixed = mm(spread.astype(BF16), value) / total
            mixed_ref[slot, :, cols] = mixed.astype(BF16)
            lse_ref[here, cols] = jnp.broadcast_to(peak + jnp.log(total), (rows, dim))


def attention_forward(z, side, start, n, heads, kv_heads, dim):
    block_rows = side.shape[0]
    rows = block_rows // n
    whole2 = lambda i, z: (0, 0)
    return call(
        functools.partial(attention_kernel, n, heads, kv_heads, dim),
        pltpu.PrefetchScalarGridSpec(
            num_scalar_prefetch=1,
            grid=(1,),
            in_specs=[
                pl.BlockSpec(side.shape, whole2),
                pl.BlockSpec((block_rows, 1), whole2),
            ],
            out_specs=[
                pl.BlockSpec((n, rows, heads * dim), lambda i, z: (0, 0, 0)),
                pl.BlockSpec((block_rows, heads * dim), whole2),
            ],
        ),
        [shape((n, rows, heads * dim), BF16), shape((block_rows, heads * dim), F32)],
        2 * block_rows * block_rows * heads * dim * 2,
        2 * side.size + 6 * block_rows * heads * dim,
    )(z, side, start)


def attention_back_kernel(
    n, heads, kv_heads, dim, z_ref, side_ref, raw_ref, gm_ref, lse_ref, start_ref, cos_ref, sin_ref,
    qg_ref, kg_ref, out_ref, gain_ref, key_acc, value_acc,
):
    block_rows = side_ref.shape[0]
    rows = block_rows // n
    group = heads // kv_heads
    q_sum = jnp.zeros((1, dim), F32)
    k_sum = jnp.zeros((1, dim), F32)
    for kv in range(kv_heads):
        key_cols = slice((heads + kv) * dim, (heads + kv + 1) * dim)
        value_cols = slice((heads + kv_heads + kv) * dim, (heads + kv_heads + kv + 1) * dim)
        key_acc[...] = jnp.zeros_like(key_acc)
        value_acc[...] = jnp.zeros_like(value_acc)
        for i in range(n):
            slot = lax.rem(z_ref[0] - i + n, n)
            keys = (i + 1) * rows
            here = slice(i * rows, (i + 1) * rows)
            key = side_ref[:keys, key_cols]
            value = side_ref[:keys, value_cols]
            visible = visible_keys(start_ref, i * rows, rows, keys)
            cosine, sine = cos_ref[here, :], sin_ref[here, :]
            for g in range(group):
                h = kv * group + g
                cols = slice(h * dim, (h + 1) * dim)
                query = side_ref[here, cols]
                grad = gm_ref[slot, :, cols]
                scores = jnp.where(visible, mm_nt(query, key), MASK_FILL)
                soft = jnp.exp(scores - lse_ref[here, cols][:, :1])
                grad_weights = mm_nt(grad, value)
                inner = jnp.sum(soft * grad_weights, axis=-1, keepdims=True)
                grad_scores = (soft * (grad_weights - inner)).astype(BF16)
                value_acc[:keys, :] += mm_tn(soft.astype(BF16), grad)
                key_acc[:keys, :] += mm_tn(grad_scores, query)
                turned = mm(grad_scores, key) * dim ** (-0.5)
                back = turned * cosine - pltpu.roll(turned, dim // 2, 1) * sine
                raw = raw_ref[here, cols].astype(F32)
                scale = inv_root_of(raw)
                normal = raw * scale
                q_sum = q_sum + jnp.sum(back * normal, axis=0, keepdims=True)
                out_ref[here, cols] = norm_back(back * qg_ref[...], normal, scale).astype(BF16)
        turned = key_acc[...]
        back = turned * cos_ref[...] - pltpu.roll(turned, dim // 2, 1) * sin_ref[...]
        raw = raw_ref[:, key_cols].astype(F32)
        scale = inv_root_of(raw)
        normal = raw * scale
        k_sum = k_sum + jnp.sum(back * normal, axis=0, keepdims=True)
        out_ref[:, key_cols] = norm_back(back * kg_ref[...], normal, scale).astype(BF16)
        out_ref[:, value_cols] = value_acc[...].astype(BF16)
    gain_ref[...] = jnp.concatenate([q_sum, k_sum, jnp.zeros((6, dim), F32)], axis=0)


def attention_backward(z, side, raw, gm, lse, start, cosine, sine, q_gain, k_gain, n, heads, kv_heads, dim):
    block_rows = side.shape[0]
    whole2 = lambda i, z: (0, 0)
    spec = lambda a: pl.BlockSpec(a.shape, (lambda i, z: (0, 0, 0)) if a.ndim == 3 else whole2)
    ins = (side, raw, gm, lse, start, cosine, sine, q_gain, k_gain)
    return call(
        functools.partial(attention_back_kernel, n, heads, kv_heads, dim),
        pltpu.PrefetchScalarGridSpec(
            num_scalar_prefetch=1,
            grid=(1,),
            in_specs=[spec(a) for a in ins],
            out_specs=[pl.BlockSpec(side.shape, whole2), pl.BlockSpec((8, dim), whole2)],
            scratch_shapes=[pltpu.VMEM((block_rows, dim), F32), pltpu.VMEM((block_rows, dim), F32)],
        ),
        [shape(side.shape, BF16), shape((8, dim), F32)],
        2 * block_rows * block_rows * heads * dim * 5,
        12 * side.size,
    )(z, *ins)


def out_kernel(n, z_ref, mixed_ref, w_ref, x_ref, gain_ref, hidden_ref, entry_ref, acc):
    k = pl.program_id(0)
    part = mm(mixed_ref[0], w_ref[...].reshape(mixed_ref.shape[2], -1))

    @pl.when(k == 0)
    def _():
        acc[...] = part + x_ref[...].astype(F32)

    @pl.when(k > 0)
    def _():
        acc[...] += part

    @pl.when(k == n - 1)
    def _():
        hidden = acc[...]
        hidden_ref[...] = hidden
        entry_ref[...] = (hidden * inv_root_of(hidden) * gain_ref[...]).astype(BF16)


def out_projection(z, mixed, w_full, x, gain, n):
    rows, width = x.shape
    cols = mixed.shape[2]
    whole = lambda k, z: (0, 0)
    return call(
        functools.partial(out_kernel, n),
        pltpu.PrefetchScalarGridSpec(
            num_scalar_prefetch=1,
            grid=(n,),
            in_specs=[
                pl.BlockSpec((1, rows, cols), lambda k, z: (k, 0, 0)),
                pl.BlockSpec(
                    (w_full.shape[0], 1, w_full.shape[2], width),
                    lambda k, z: (0, lax.rem(z[0] - k + n, n), 0, 0),
                ),
                pl.BlockSpec((rows, width), whole),
                pl.BlockSpec((1, width), whole),
            ],
            out_specs=[pl.BlockSpec((rows, width), whole), pl.BlockSpec((rows, width), whole)],
            scratch_shapes=[pltpu.VMEM((rows, width), F32)],
        ),
        [shape((rows, width), F32), shape((rows, width), BF16)],
        2 * rows * width * cols * n,
        2 * w_full.size + 10 * rows * width,
    )(z, mixed, w_full, x, gain)


def mlp_kernel(tiles, sid_ref, x_ref, go_ref, wg_ref, wu_ref, wd_ref, *refs):
    active_ref, gate_grad_ref, up_grad_ref, down_ref, inner_ref, down_acc, inner_acc = refs[-7:]
    j = pl.program_id(0)
    x = x_ref[...]
    gate = mm(x, wg_ref[...])
    up = mm(x, wu_ref[...])
    sigmoid = jax.nn.sigmoid(gate)
    silu = gate * sigmoid
    active = (silu * up).astype(BF16)
    active_ref[...] = active
    grad_active = mm_nt(go_ref[...], wd_ref[...])
    gate_grad = (grad_active * up * sigmoid * (1.0 + gate * (1.0 - sigmoid))).astype(BF16)
    up_grad = (grad_active * silu).astype(BF16)
    gate_grad_ref[...] = gate_grad
    up_grad_ref[...] = up_grad
    inner = mm_nt(gate_grad, wg_ref[...]) + mm_nt(up_grad, wu_ref[...])
    down = mm(active, wd_ref[...])

    @pl.when(j == 0)
    def _():
        inner_acc[...] = inner
        down_acc[...] = down

    @pl.when(j > 0)
    def _():
        inner_acc[...] += inner
        down_acc[...] += down

    @pl.when(j == tiles - 1)
    def _():
        inner_ref[...] = inner_acc[...].astype(BF16)
        down_ref[...] = down_acc[...].astype(BF16)


def mlp_shard(sid, x, grad_all, w_gate, w_up, w_down, kept):
    rows, width = x.shape
    block_rows = grad_all.shape[0]
    units = w_gate.shape[1]
    tile = next(t for t in (512, 384, 256, 128) if units % t == 0)
    tiles = units // tile
    whole = lambda j, sid: (0, 0)
    mine = lambda j, sid: (sid[0], 0)
    tiled = lambda j, sid: (sid[0], j)
    in_specs = [
        pl.BlockSpec((rows, width), whole),
        pl.BlockSpec((rows, width), mine),
        pl.BlockSpec((width, tile), lambda j, sid: (0, j)),
        pl.BlockSpec((width, tile), lambda j, sid: (0, j)),
        pl.BlockSpec((tile, width), lambda j, sid: (j, 0)),
    ]
    args = [sid, x, grad_all, w_gate, w_up, w_down]
    aliases = {}
    if kept is not None:
        for j, array in enumerate(kept):
            aliases[len(args)] = j
            args.append(array)
            in_specs.append(pl.BlockSpec(memory_space=pl.ANY))
    return call(
        functools.partial(mlp_kernel, tiles),
        pltpu.PrefetchScalarGridSpec(
            num_scalar_prefetch=1,
            grid=(tiles,),
            in_specs=in_specs,
            out_specs=[
                pl.BlockSpec((rows, tile), tiled),
                pl.BlockSpec((rows, tile), tiled),
                pl.BlockSpec((rows, tile), tiled),
                pl.BlockSpec((rows, width), mine),
                pl.BlockSpec((rows, width), whole),
            ],
            scratch_shapes=[pltpu.VMEM((rows, width), F32), pltpu.VMEM((rows, width), F32)],
        ),
        [
            shape((block_rows, units), BF16),
            shape((block_rows, units), BF16),
            shape((block_rows, units), BF16),
            shape((block_rows, width), BF16),
            shape((rows, width), BF16),
        ],
        2 * rows * width * units * 6,
        2 * (3 * width * units + 3 * rows * units + 4 * rows * width),
        aliases,
    )(*args)


def mid_kernel(n, z_ref, got_ref, own_ref, go_ref, hidden_ref, gain_ref, w_ref, gm_ref, gh_ref, mid_ref, part_ref):
    k = pl.program_id(0)

    @pl.when(k == 0)
    def _():
        hidden = hidden_ref[...]
        scale = inv_root_of(hidden)
        normal = hidden * scale
        inner = got_ref[...].astype(F32) + own_ref[...].astype(F32)
        part_ref[...] = jnp.sum(inner * normal, axis=0, keepdims=True)
        grad_hidden = go_ref[...].astype(F32) + norm_back(inner * gain_ref[...], normal, scale)
        gh_ref[...] = grad_hidden
        mid_ref[...] = grad_hidden.astype(BF16)

    gm_ref[0] = mm_nt(mid_ref[...], w_ref[...].reshape(gm_ref.shape[2], -1)).astype(BF16)


def mid_stage(z, got, own, go, hidden, gain, w_full, n):
    rows, width = go.shape
    cols = w_full.shape[0] * w_full.shape[2]
    whole = lambda k, z: (0, 0)
    return call(
        functools.partial(mid_kernel, n),
        pltpu.PrefetchScalarGridSpec(
            num_scalar_prefetch=1,
            grid=(n,),
            in_specs=[
                pl.BlockSpec((rows, width), whole),
                pl.BlockSpec((rows, width), whole),
                pl.BlockSpec((rows, width), whole),
                pl.BlockSpec((rows, width), whole),
                pl.BlockSpec((1, width), whole),
                pl.BlockSpec(
                    (w_full.shape[0], 1, w_full.shape[2], width),
                    lambda k, z: (0, lax.rem(z[0] + k, n), 0, 0),
                ),
            ],
            out_specs=[
                pl.BlockSpec((1, rows, cols), lambda k, z: (k, 0, 0)),
                pl.BlockSpec((rows, width), whole),
                pl.BlockSpec((rows, width), whole),
                pl.BlockSpec((1, width), whole),
            ],
        ),
        [
            shape((n, rows, cols), BF16),
            shape((rows, width), F32),
            shape((rows, width), BF16),
            shape((1, width), F32),
        ],
        2 * rows * width * cols * n,
        2 * w_full.size + 20 * rows * width,
    )(z, got, own, go, hidden, gain, w_full)


def out_weight_kernel(z_ref, mixed_ref, mid_ref, out_ref):
    grad = mm_tn(mixed_ref[0], mid_ref[...]).astype(BF16)
    cols = out_ref.shape[3]
    for b in range(out_ref.shape[0]):
        out_ref[b, 0] = grad[:, b * cols : (b + 1) * cols]


def out_weight_grad(z, mixed, mid, n, batches):
    rows, width = mid.shape
    cols = mixed.shape[2]
    return call(
        out_weight_kernel,
        pltpu.PrefetchScalarGridSpec(
            num_scalar_prefetch=1,
            grid=(n,),
            in_specs=[
                pl.BlockSpec((1, rows, cols), lambda k, z: (k, 0, 0)),
                pl.BlockSpec((rows, width), lambda k, z: (0, 0)),
            ],
            out_specs=pl.BlockSpec(
                (batches, 1, cols, width // batches),
                lambda k, z: (0, lax.rem(z[0] - k + n, n), 0, 0),
            ),
        ),
        shape((batches, n, cols, width // batches), BF16),
        2 * rows * width * cols * n,
        2 * n * cols * width,
    )(z, mixed, mid)


def qkv_weight_kernel(entry_ref, grad_ref, w_ref, out_ref, part_ref):
    grad = mm_tn(entry_ref[...], grad_ref[...])
    out_ref[...] = grad.astype(BF16)
    both = grad * w_ref[...].astype(F32)
    lanes = part_ref.shape[1]
    total = both[:, :lanes]
    for first in range(lanes, both.shape[1], lanes):
        total = total + both[:, first : first + lanes]

    @pl.when(pl.program_id(0) == 0)
    def _():
        part_ref[...] = total

    @pl.when(pl.program_id(0) > 0)
    def _():
        part_ref[...] += total


def qkv_weight_grad(entry, grads, w_qkv):
    block_rows, width = entry.shape
    cols = grads.shape[1]
    tile = 256
    return call(
        qkv_weight_kernel,
        pltpu.PrefetchScalarGridSpec(
            num_scalar_prefetch=0,
            grid=(cols // tile,),
            in_specs=[
                pl.BlockSpec((block_rows, width), lambda j: (0, 0)),
                pl.BlockSpec((block_rows, tile), lambda j: (0, j)),
                pl.BlockSpec((width, tile), lambda j: (0, j)),
            ],
            out_specs=[
                pl.BlockSpec((width, tile), lambda j: (0, j)),
                pl.BlockSpec((width, 128), lambda j: (0, 0)),
            ],
        ),
        [shape((width, cols), BF16), shape((width, 128), F32)],
        2 * block_rows * width * cols,
        2 * (block_rows * width + block_rows * cols + 2 * width * cols),
    )(entry, grads, w_qkv)


def exchange(value, axis, step):
    size = lax.axis_size(axis)
    return lax.ppermute(value, axis, [(i, i ^ step) for i in range(size)])


def total_over(value, axis):
    step = 1
    while step < lax.axis_size(axis):
        value = value + exchange(value, axis, step)
        step *= 2
    return value


def halve(value, axes, bits, bit):
    own = lax.rem(lax.div(lax.axis_index("dp"), 1 << bit), 2)
    at = axes.index(bit)
    sent = lax.dynamic_index_in_dim(value, 1 - own, at, False).astype(BF16)
    kept = lax.dynamic_index_in_dim(value, own, at, False)
    total = kept.astype(F32) + exchange(sent, "dp", 1 << bit).astype(F32)
    return total, axes[:at] + axes[at + 1 :]


def halved_over_dp(value):
    batches = value.shape[0]
    bits = batches.bit_length() - 1
    axes = list(range(bits))[::-1]
    value = value.reshape((2,) * bits + value.shape[1:])
    value, axes = halve(value, axes, bits, 0)
    middle = value.shape[-1] // 2
    results = []
    for part, order in ((value[..., :middle], axes[::-1]), (value[..., middle:], axes)):
        left = axes
        for bit in order:
            part, left = halve(part, left, bits, bit)
        results.append(part)
    return jnp.concatenate(results, axis=-1)


def line_sum(value, z, n):
    rows = value.shape[0] // n
    shard = lambda d: lax.dynamic_slice_in_dim(value, jnp.clip(z + d, 0, n - 1) * rows, rows, 0)
    right = left = None
    for s in range(1, n):
        far = n - s
        to_right, to_left = shard(far), shard(-far)
        if right is not None:
            to_right = (to_right.astype(F32) + right.astype(F32)).astype(BF16)
            to_left = (to_left.astype(F32) + left.astype(F32)).astype(BF16)
        right = lax.ppermute(to_right, "tensor", [(i, i + 1) for i in range(s)])
        left = lax.ppermute(to_left, "tensor", [(i, i - 1) for i in range(n - s, n)])
    return shard(0).astype(F32) + right.astype(F32) + left.astype(F32)


def local(
    tokens,
    seq_lengths,
    attn_gain,
    mlp_gain,
    q_gain,
    k_gain,
    w_query,
    key_weight,
    value_weight,
    w_out,
    w_gate,
    w_up,
    w_down,
    out_grad,
):
    n = lax.axis_size("tensor")
    batches = lax.axis_size("dp")
    rows, width = tokens.shape
    block_rows = rows * n
    dim = q_gain.shape[0]
    heads = w_query.shape[1] // dim
    kv_heads = key_weight.shape[1] // dim
    z = lax.axis_index("tensor").astype(jnp.int32)
    zs = z.reshape(1)
    ring = [(i, (i + 1) % n) for i in range(n)]
    shift = lambda v, d=1: lax.ppermute(v, "tensor", [(i, (i + d) % n) for i in range(n)])
    shard_of = lambda s: lax.rem(z - s + n, n).reshape(1)

    own_rows = w_out.shape[0] // batches
    piece = lax.dynamic_slice_in_dim(w_out, lax.axis_index("dp") * own_rows, own_rows, 0)
    piece = lax.all_gather(piece, "tensor", axis=0, tiled=False)
    w_out_full = lax.all_gather(piece, "dp", axis=0, tiled=False)

    offset, position = positions_of(seq_lengths[0], block_rows)
    start = offset[:, None]
    cosine, sine = rope_tables(position, dim)
    w_qkv = jnp.concatenate([w_query, key_weight, value_weight], axis=1)
    gain_one, gain_two = attn_gain[None, :], mlp_gain[None, :]
    qg, kg = q_gain[None, :], k_gain[None, :]

    kept = None
    block = tokens
    for s in range(n):
        later = shift(block) if s < n - 1 else None
        kept = qkv_shard(
            shard_of(s), block, gain_one, w_qkv, cosine, sine, qg, kg, heads, kv_heads, dim, block_rows, kept
        )
        last, block = block, later
    entry_all, side, raw = kept

    later_grad, _ = lax.optimization_barrier((out_grad, last))
    grad_all = lax.all_gather(later_grad, "tensor", axis=0, tiled=True)

    mixed, lse = attention_forward(zs, side, start, n, heads, kv_heads, dim)
    mixed = jnp.stack([mixed[0]] + [shift(mixed[d], d) for d in range(1, n)])
    hidden, mlp_entry = out_projection(zs, mixed, w_out_full, tokens, gain_two, n)

    kept = None
    block = mlp_entry
    blocks, partials = [], []
    for s in range(n):
        later = shift(block) if s < n - 1 else None
        *kept, partial = mlp_shard(shard_of(s), block, grad_all, w_gate, w_up, w_down, kept)
        blocks.append(block)
        partials.append(partial)
        block = later
    active, gate_grad, up_grad, down = kept

    moving = partials[1]
    for s in range(2, n + 1):
        moving = shift(moving)
        if s < n:
            moving = (moving.astype(F32) + partials[s].astype(F32)).astype(BF16)

    mlp_all = jnp.zeros((block_rows, width), BF16)
    for s in range(n):
        mlp_all = lax.dynamic_update_slice_in_dim(mlp_all, blocks[s], shard_of(s)[0] * rows, 0)
    w_down_grad = mm_tn(active, grad_all).astype(BF16)
    w_gate_grad = mm_tn(mlp_all, gate_grad).astype(BF16)
    w_up_grad = mm_tn(mlp_all, up_grad).astype(BF16)
    moving, w_down_grad, w_gate_grad, w_up_grad = lax.optimization_barrier(
        (moving, w_down_grad, w_gate_grad, w_up_grad)
    )

    gm, grad_hidden, grad_mid, mlp_part = mid_stage(
        zs, moving, partials[0], out_grad, hidden, gain_two, w_out_full, n
    )
    gm, down = lax.optimization_barrier((gm, down))
    ffn = line_sum(down, z, n)
    output = (hidden + ffn).astype(BF16)
    gm = jnp.stack([gm[0]] + [shift(gm[d], d) for d in range(1, n)])
    grads, gain_parts = attention_backward(
        zs, side, raw, gm, lse, start, cosine, sine, qg, kg, n, heads, kv_heads, dim
    )
    w_out_grad = out_weight_grad(zs, mixed, grad_mid, n, batches)

    def entry_part(s):
        mine = lax.dynamic_slice_in_dim(grads, shard_of(s)[0] * rows, rows, 0)
        return mm_nt(mine, w_qkv)

    moving = entry_part(1).astype(BF16)
    for s in range(2, n + 1):
        moving = shift(moving)
        if s < n:
            moving = (moving.astype(F32) + entry_part(s)).astype(BF16)
    grad_entry = moving.astype(F32) + entry_part(0)
    w_qkv_grad, attn_lanes = qkv_weight_grad(entry_all, grads, w_qkv)

    x = tokens.astype(F32)
    scale = inv_root_of(x)
    token_grad = (grad_hidden + norm_back(grad_entry * attn_gain, x * scale, scale)).astype(BF16)

    attn_part = jnp.sum(attn_lanes, axis=1) / attn_gain
    totals = jnp.concatenate([attn_part, mlp_part[0], gain_parts[0], gain_parts[1]])[None, :]
    totals = total_over(total_over(totals, "dp"), "tensor")[0]
    attn_gain_grad = totals[:width]
    mlp_gain_grad = totals[width : 2 * width]
    q_gain_grad = totals[2 * width : 2 * width + dim]
    k_gain_grad = totals[2 * width + dim :]

    over_dp = lambda g, d: lax.psum_scatter(g, "dp", scatter_dimension=d, tiled=True)
    w_down_grad = over_dp(w_down_grad, 1).astype(F32)
    w_gate_grad = over_dp(w_gate_grad, 0).astype(F32)
    w_up_grad = over_dp(w_up_grad, 0).astype(F32)
    w_out_grad = halved_over_dp(w_out_grad).astype(BF16)
    pieces = [lax.dynamic_index_in_dim(w_out_grad, lax.rem(z + d, n), 0, False) for d in range(n)]
    w_out_grad = pieces[0].astype(F32)
    for d in range(1, n):
        w_out_grad = w_out_grad + shift(pieces[d], d).astype(F32)
    w_qkv_grad = halved_over_dp(
        w_qkv_grad.reshape(batches, width // batches, w_qkv_grad.shape[1])
    )
    a, b = heads * dim, (heads + kv_heads) * dim
    return (
        output,
        token_grad,
        attn_gain_grad,
        mlp_gain_grad,
        q_gain_grad,
        k_gain_grad,
        w_qkv_grad[:, :a],
        w_qkv_grad[:, a:b],
        w_qkv_grad[:, b:],
        w_out_grad,
        w_gate_grad,
        w_up_grad,
        w_down_grad,
    )


def solution(mesh):
    return jax.shard_map(
        local,
        mesh=mesh,
        in_specs=(
            P(("dp", "tensor"), None),
            P("dp", None),
            P(),
            P(),
            P(),
            P(),
            P(None, "tensor"),
            P(None, "tensor"),
            P(None, "tensor"),
            P("tensor", None),
            P(None, "tensor"),
            P(None, "tensor"),
            P("tensor", None),
            P(("dp", "tensor"), None),
        ),
        out_specs=(
            P(("dp", "tensor"), None),
            P(("dp", "tensor"), None),
            P(),
            P(),
            P(),
            P(),
            P("dp", "tensor"),
            P("dp", "tensor"),
            P("dp", "tensor"),
            P("tensor", "dp"),
            P("dp", "tensor"),
            P("dp", "tensor"),
            P("tensor", "dp"),
        ),
        check_vma=False,
    )
```

```python
import functools

import jax
import jax.numpy as jnp
from jax import lax
from jax.experimental import pallas as pl
from jax.experimental.pallas import tpu as pltpu
from jax.sharding import Mesh, PartitionSpec as P

NORM_EPSILON = 1e-06
ROPE_BASE = 1000000.0
MASK_FILL = -1e30
VMEM_BYTES = 52 * 1024 * 1024
F32 = jnp.float32
BF16 = jnp.bfloat16
DP = ("chip", "core")
COST = 1000

NT = (((1,), (1,)), ((), ()))
TN = (((0,), (0,)), ((), ()))


def mm(a, b):
    return jnp.dot(a, b, preferred_element_type=F32)


def mm_nt(a, b):
    return lax.dot_general(a, b, NT, preferred_element_type=F32)


def mm_tn(a, b):
    return lax.dot_general(a, b, TN, preferred_element_type=F32)


def inv_root_of(values):
    return lax.rsqrt(jnp.mean(values * values, axis=-1, keepdims=True) + NORM_EPSILON)


def norm_back(grad_normed, normal, inv_root):
    return inv_root * (
        grad_normed - normal * jnp.mean(grad_normed * normal, axis=-1, keepdims=True)
    )


def call(kernel, grid_spec, out_shape, flops, nbytes, aliases=None):
    return pl.pallas_call(
        kernel,
        grid_spec=grid_spec,
        out_shape=out_shape,
        input_output_aliases=aliases or {},
        compiler_params=pltpu.CompilerParams(vmem_limit_bytes=VMEM_BYTES),
        cost_estimate=pl.CostEstimate(flops=flops // COST, bytes_accessed=nbytes // COST, transcendentals=0),
    )


def shape(dims, dtype):
    return jax.ShapeDtypeStruct(dims, dtype)


def positions_of(lengths, count_of_rows):
    seq_ends = jnp.cumsum(lengths, dtype=jnp.int32)
    starts = seq_ends - lengths
    place_index = jnp.arange(count_of_rows, dtype=jnp.int32)
    segment = jnp.sum(
        (place_index[:, None] >= seq_ends[None, :]).astype(jnp.int32), axis=1, dtype=jnp.int32
    )
    belongs = segment[:, None] == jnp.arange(lengths.shape[0], dtype=jnp.int32)[None, :]
    offset = jnp.sum(jnp.where(belongs, starts[None, :], 0), axis=1, dtype=jnp.int32)
    return (offset, place_index - offset)


def rope_tables(position, head_width):
    half_width = head_width // 2
    frequency = ROPE_BASE ** (-2.0 * jnp.arange(half_width, dtype=F32) / head_width)
    angles = position.astype(F32)[:, None] * frequency[None, :]
    cosine, sine = jnp.cos(angles), jnp.sin(angles)
    return (
        jnp.concatenate([cosine, cosine], axis=1),
        jnp.concatenate([-sine, sine], axis=1),
    )


def qkv_kernel(heads, kv_heads, dim, sid_ref, x_ref, gain_ref, w_ref, cos_ref, sin_ref, qg_ref, kg_ref, *refs):
    entry_ref, side_ref, raw_ref = refs[-3:]
    x = x_ref[...].astype(F32)
    entry = (x * inv_root_of(x) * gain_ref[...]).astype(BF16)
    entry_ref[...] = entry
    both = mm(entry, w_ref[...])
    cosine, sine = cos_ref[...], sin_ref[...]
    for h in range(heads + kv_heads):
        cols = slice(h * dim, (h + 1) * dim)
        raw = both[:, cols]
        raw_ref[:, cols] = raw.astype(BF16)
        gain = qg_ref[...] if h < heads else kg_ref[...]
        u = raw * inv_root_of(raw) * gain
        turned = u * cosine + pltpu.roll(u, dim // 2, 1) * sine
        if h < heads:
            turned = turned * dim ** (-0.5)
        side_ref[:, cols] = turned.astype(BF16)
    rest = slice((heads + kv_heads) * dim, (heads + 2 * kv_heads) * dim)
    side_ref[:, rest] = both[:, rest].astype(BF16)


def qkv_shard(sid, x, gain, w_qkv, cosine, sine, q_gain, k_gain, heads, kv_heads, dim, block_rows, kept):
    rows, width = x.shape
    cols = w_qkv.shape[1]
    raw_cols = (heads + kv_heads) * dim
    whole = lambda i, sid: (0, 0)
    mine = lambda i, sid: (sid[0], 0)
    in_specs = [
        pl.BlockSpec((rows, width), whole),
        pl.BlockSpec((1, width), whole),
        pl.BlockSpec((width, cols), whole),
        pl.BlockSpec((rows, dim), mine),
        pl.BlockSpec((rows, dim), mine),
        pl.BlockSpec((1, dim), whole),
        pl.BlockSpec((1, dim), whole),
    ]
    args = [sid, x, gain, w_qkv, cosine, sine, q_gain, k_gain]
    aliases = {}
    if kept is not None:
        for j, array in enumerate(kept):
            aliases[len(args)] = j
            args.append(array)
            in_specs.append(pl.BlockSpec(memory_space=pl.ANY))
    return call(
        functools.partial(qkv_kernel, heads, kv_heads, dim),
        pltpu.PrefetchScalarGridSpec(
            num_scalar_prefetch=1,
            grid=(1,),
            in_specs=in_specs,
            out_specs=[
                pl.BlockSpec((rows, width), mine),
                pl.BlockSpec((rows, cols), mine),
                pl.BlockSpec((rows, raw_cols), mine),
            ],
        ),
        [
            shape((block_rows, width), BF16),
            shape((block_rows, cols), BF16),
            shape((block_rows, raw_cols), BF16),
        ],
        2 * rows * width * cols,
        2 * (2 * rows * width + width * cols + 2 * rows * cols),
        aliases,
    )(*args)


def visible_keys(start_ref, first_row, rows, keys):
    key = lax.broadcasted_iota(jnp.int32, (keys, rows), 0)
    query = first_row + lax.broadcasted_iota(jnp.int32, (keys, rows), 1)
    return (key <= query) & (key >= start_ref[:, first_row : first_row + rows])


def attention_kernel(n, heads, kv_heads, dim, z_ref, side_ref, start_ref, mixed_ref, lse_ref):
    rows = side_ref.shape[0] // n
    group = heads // kv_heads
    for i in range(n):
        slot = lax.rem(i - z_ref[0] + n, n)
        keys = (i + 1) * rows
        here = slice(i * rows, (i + 1) * rows)
        visible = visible_keys(start_ref, i * rows, rows, keys)
        for h in range(heads):
            kv = h // group
            key = side_ref[:keys, (heads + kv) * dim : (heads + kv + 1) * dim]
            value = side_ref[
                :keys, (heads + kv_heads + kv) * dim : (heads + kv_heads + kv + 1) * dim
            ]
            cols = slice(h * dim, (h + 1) * dim)
            scores = jnp.where(visible, mm_nt(key, side_ref[here, cols]), MASK_FILL)
            peak = jnp.max(scores, axis=0, keepdims=True)
            spread = jnp.exp(scores - peak)
            total = jnp.sum(spread, axis=0, keepdims=True)
            mixed = mm_tn(value, spread.astype(BF16)) / total
            mixed_ref[slot, :, cols] = mixed.T.astype(BF16)
            lse_ref[h : h + 1, here] = peak + jnp.log(total)


def attention_forward(z, side, start, n, heads, kv_heads, dim):
    block_rows = side.shape[0]
    rows = block_rows // n
    whole2 = lambda i, z: (0, 0)
    return call(
        functools.partial(attention_kernel, n, heads, kv_heads, dim),
        pltpu.PrefetchScalarGridSpec(
            num_scalar_prefetch=1,
            grid=(1,),
            in_specs=[
                pl.BlockSpec(side.shape, whole2),
                pl.BlockSpec((1, block_rows), whole2),
            ],
            out_specs=[
                pl.BlockSpec((n, rows, heads * dim), lambda i, z: (0, 0, 0)),
                pl.BlockSpec((heads, block_rows), whole2),
            ],
        ),
        [shape((n, rows, heads * dim), BF16), shape((heads, block_rows), F32)],
        2 * block_rows * block_rows * heads * dim * 2,
        2 * side.size + 6 * block_rows * heads * dim,
    )(z, side, start)


def attention_back_kernel(n, heads, kv_heads, dim, z_ref, *refs):
    gm_refs = refs[:n]
    side_ref, raw_ref, lse_ref, start_ref, cos_ref, sin_ref, qg_ref, kg_ref = refs[n : n + 8]
    out_ref, gain_ref, gm_ref, key_acc, value_acc = refs[n + 8 :]
    block_rows = side_ref.shape[0]
    rows = block_rows // n
    group = heads // kv_heads
    q_sum = jnp.zeros((1, dim), F32)
    k_sum = jnp.zeros((1, dim), F32)
    for slot, ref in enumerate(gm_refs):
        gm_ref[slot] = ref[...]
    for kv in range(kv_heads):
        key_cols = slice((heads + kv) * dim, (heads + kv + 1) * dim)
        value_cols = slice((heads + kv_heads + kv) * dim, (heads + kv_heads + kv + 1) * dim)
        key_acc[...] = jnp.zeros_like(key_acc)
        value_acc[...] = jnp.zeros_like(value_acc)
        for i in range(n):
            slot = lax.rem(z_ref[0] - i + n, n)
            keys = (i + 1) * rows
            here = slice(i * rows, (i + 1) * rows)
            key = side_ref[:keys, key_cols]
            value = side_ref[:keys, value_cols]
            visible = visible_keys(start_ref, i * rows, rows, keys)
            cosine, sine = cos_ref[here, :], sin_ref[here, :]
            for g in range(group):
                h = kv * group + g
                cols = slice(h * dim, (h + 1) * dim)
                query = side_ref[here, cols]
                grad = gm_ref[slot, :, cols]
                scores = jnp.where(visible, mm_nt(key, query), MASK_FILL)
                soft = jnp.exp(scores - lse_ref[h : h + 1, here])
                grad_weights = mm_nt(value, grad)
                inner = jnp.sum(soft * grad_weights, axis=0, keepdims=True)
                grad_scores = (soft * (grad_weights - inner)).astype(BF16)
                value_acc[:keys, :] += mm(soft.astype(BF16), grad)
                key_acc[:keys, :] += mm(grad_scores, query)
                turned = mm_tn(key, grad_scores).T * dim ** (-0.5)
                back = turned * cosine - pltpu.roll(turned, dim // 2, 1) * sine
                raw = raw_ref[here, cols].astype(F32)
                scale = inv_root_of(raw)
                normal = raw * scale
                q_sum = q_sum + jnp.sum(back * normal, axis=0, keepdims=True)
                out_ref[here, cols] = norm_back(back * qg_ref[...], normal, scale).astype(BF16)
        turned = key_acc[...]
        back = turned * cos_ref[...] - pltpu.roll(turned, dim // 2, 1) * sin_ref[...]
        raw = raw_ref[:, key_cols].astype(F32)
        scale = inv_root_of(raw)
        normal = raw * scale
        k_sum = k_sum + jnp.sum(back * normal, axis=0, keepdims=True)
        out_ref[:, key_cols] = norm_back(back * kg_ref[...], normal, scale).astype(BF16)
        out_ref[:, value_cols] = value_acc[...].astype(BF16)
    gain_ref[...] = jnp.concatenate([q_sum, k_sum, jnp.zeros((6, dim), F32)], axis=0)


def attention_backward(z, gm, side, raw, lse, start, cosine, sine, q_gain, k_gain, heads, kv_heads, dim):
    n = len(gm)
    block_rows = side.shape[0]
    whole2 = lambda i, z: (0, 0)
    ins = (*gm, side, raw, lse, start, cosine, sine, q_gain, k_gain)
    return call(
        functools.partial(attention_back_kernel, n, heads, kv_heads, dim),
        pltpu.PrefetchScalarGridSpec(
            num_scalar_prefetch=1,
            grid=(1,),
            in_specs=[pl.BlockSpec(a.shape, whole2) for a in ins],
            out_specs=[pl.BlockSpec(side.shape, whole2), pl.BlockSpec((8, dim), whole2)],
            scratch_shapes=[
                pltpu.VMEM((n,) + gm[0].shape, BF16),
                pltpu.VMEM((block_rows, dim), F32),
                pltpu.VMEM((block_rows, dim), F32),
            ],
        ),
        [shape(side.shape, BF16), shape((8, dim), F32)],
        2 * block_rows * block_rows * heads * dim * 5,
        12 * side.size,
    )(z, *ins)


def column_block(place_ref, k, other, cols):
    block = 2 * lax.bitwise_xor(place_ref[1], k) + (1 - place_ref[2] if other else place_ref[2])
    return pl.ds(pl.multiple_of(block * cols, cols), cols)


def out_kernel(n, chips, place_ref, *refs):
    mixed_refs = refs[:n]
    own_ref, other_ref, x_ref, gain_ref, hidden_ref, entry_ref, acc = refs[n:]
    k = pl.program_id(0)
    for other, w_ref in enumerate((own_ref, other_ref)):
        part = mm(mixed_refs[0][...], w_ref[0, place_ref[0]])
        for s in range(1, n):
            part = part + mm(mixed_refs[s][...], w_ref[0, lax.rem(place_ref[0] - s + n, n)])
        acc[:, column_block(place_ref, k, other, part.shape[1])] = part

    @pl.when(k == chips - 1)
    def _():
        hidden = acc[...] + x_ref[...].astype(F32)
        hidden_ref[...] = hidden
        entry_ref[...] = (hidden * inv_root_of(hidden) * gain_ref[...]).astype(BF16)


def out_projection(place, mixed, w_own, w_other, x, gain, n):
    rows, width = x.shape
    chips = w_own.shape[0]
    whole = lambda k, place: (0, 0)
    block = pl.BlockSpec((1,) + w_own.shape[1:], lambda k, place: (k, 0, 0, 0))
    return call(
        functools.partial(out_kernel, n, chips),
        pltpu.PrefetchScalarGridSpec(
            num_scalar_prefetch=1,
            grid=(chips,),
            in_specs=[pl.BlockSpec(mixed[0].shape, whole)] * n
            + [
                block,
                block,
                pl.BlockSpec((rows, width), whole),
                pl.BlockSpec((1, width), whole),
            ],
            out_specs=[pl.BlockSpec((rows, width), whole), pl.BlockSpec((rows, width), whole)],
            scratch_shapes=[pltpu.VMEM((rows, width), F32)],
        ),
        [shape((rows, width), F32), shape((rows, width), BF16)],
        4 * rows * w_own.size,
        4 * w_own.size + 10 * rows * width,
    )(place, *mixed, w_own, w_other, x, gain)


def mlp_kernel(tiles, sid_ref, x_ref, go_ref, wg_ref, wu_ref, wd_ref, *refs):
    active_ref, gate_grad_ref, up_grad_ref, copy_ref, down_ref, inner_ref, down_acc, inner_acc = refs[-8:]
    j = pl.program_id(0)
    x = x_ref[...]
    gate = mm(x, wg_ref[...])
    up = mm(x, wu_ref[...])
    sigmoid = jax.nn.sigmoid(gate)
    silu = gate * sigmoid
    active = (silu * up).astype(BF16)
    active_ref[...] = active
    grad_active = mm_nt(go_ref[...], wd_ref[...])
    gate_grad = (grad_active * up * sigmoid * (1.0 + gate * (1.0 - sigmoid))).astype(BF16)
    up_grad = (grad_active * silu).astype(BF16)
    gate_grad_ref[...] = gate_grad
    up_grad_ref[...] = up_grad
    inner = mm_nt(gate_grad, wg_ref[...]) + mm_nt(up_grad, wu_ref[...])
    down = mm(active, wd_ref[...])

    @pl.when(j == 0)
    def _():
        copy_ref[...] = x
        inner_acc[...] = inner
        down_acc[...] = down

    @pl.when(j > 0)
    def _():
        inner_acc[...] += inner
        down_acc[...] += down

    @pl.when(j == tiles - 1)
    def _():
        inner_ref[...] = inner_acc[...].astype(BF16)
        down_ref[...] = down_acc[...].astype(BF16)


def mlp_shard(sid, x, grads, weights, kept, block_rows):
    w_gate, w_up, w_down = weights
    rows, width = x.shape
    units = w_gate.shape[1]
    tile = next(t for t in (512, 384, 256, 128) if units % t == 0)
    tiles = units // tile
    whole = pl.BlockSpec((rows, width), lambda j, sid: (0, 0))
    mine = pl.BlockSpec((rows, width), lambda j, sid: (sid[0], 0))
    tiled = pl.BlockSpec((rows, tile), lambda j, sid: (sid[0], j))
    column = pl.BlockSpec((width, tile), lambda j, sid: (0, j))
    in_specs = [
        whole,
        whole if grads.shape[0] == rows else mine,
        column,
        column,
        pl.BlockSpec((tile, width), lambda j, sid: (j, 0)),
    ]
    args = [sid.reshape(1), x, grads, w_gate, w_up, w_down]
    aliases = {}
    if kept is not None:
        for j, array in enumerate(kept):
            aliases[len(args)] = j
            args.append(array)
            in_specs.append(pl.BlockSpec(memory_space=pl.ANY))
    *kept, down, inner = call(
        functools.partial(mlp_kernel, tiles),
        pltpu.PrefetchScalarGridSpec(
            num_scalar_prefetch=1,
            grid=(tiles,),
            in_specs=in_specs,
            out_specs=[tiled] * 3 + [mine] + [whole] * 2,
            scratch_shapes=[pltpu.VMEM((rows, width), F32), pltpu.VMEM((rows, width), F32)],
        ),
        [shape((block_rows, units), BF16)] * 3
        + [shape((block_rows, width), BF16)]
        + [shape((rows, width), BF16)] * 2,
        2 * rows * width * units * 6,
        2 * (3 * width * units + 3 * rows * units + 5 * rows * width),
        aliases,
    )(*args)
    return kept, down, inner


def mid_kernel(n, chips, place_ref, own_part_ref, go_ref, hidden_ref, gain_ref, own_ref, other_ref, *refs):
    got_refs = refs[:-5]
    gm_ref, gh_ref, mid_ref, part_ref, acc = refs[-5:]
    k = pl.program_id(0)

    @pl.when(k == 0)
    def _():
        hidden = hidden_ref[...]
        scale = inv_root_of(hidden)
        normal = hidden * scale
        inner = own_part_ref[...].astype(F32)
        for ref in got_refs:
            inner = inner + ref[...].astype(F32)
        part_ref[...] = jnp.sum(inner * normal, axis=0, keepdims=True)
        grad_hidden = go_ref[...].astype(F32) + norm_back(inner * gain_ref[...], normal, scale)
        gh_ref[...] = grad_hidden
        mid_ref[...] = grad_hidden.astype(BF16)
        acc[...] = jnp.zeros_like(acc)

    cols = own_ref.shape[3]
    own = mid_ref[:, column_block(place_ref, k, False, cols)]
    other = mid_ref[:, column_block(place_ref, k, True, cols)]
    for s in range(n):
        t = lax.rem(place_ref[0] + s, n)
        acc[s] += mm_nt(own, own_ref[0, t]) + mm_nt(other, other_ref[0, t])

    @pl.when(k == chips - 1)
    def _():
        gm_ref[...] = acc[...].astype(BF16)


def mid_stage(place, own, got, go, hidden, gain, w_own, w_other, n):
    rows, width = go.shape
    chips, _, heads_cols, _ = w_own.shape
    whole = pl.BlockSpec((rows, width), lambda k, place: (0, 0))
    line = pl.BlockSpec((1, width), lambda k, place: (0, 0))
    block = pl.BlockSpec((1,) + w_own.shape[1:], lambda k, place: (k, 0, 0, 0))
    return call(
        functools.partial(mid_kernel, n, chips),
        pltpu.PrefetchScalarGridSpec(
            num_scalar_prefetch=1,
            grid=(chips,),
            in_specs=[whole, whole, whole, line, block, block] + [whole] * len(got),
            out_specs=[
                pl.BlockSpec((n, rows, heads_cols), lambda k, place: (0, 0, 0)),
                whole,
                whole,
                line,
            ],
            scratch_shapes=[pltpu.VMEM((n, rows, heads_cols), F32)],
        ),
        [
            shape((n, rows, heads_cols), BF16),
            shape((rows, width), F32),
            shape((rows, width), BF16),
            shape((1, width), F32),
        ],
        4 * rows * w_own.size,
        4 * w_own.size + 20 * rows * width,
    )(place, own, go, hidden, gain, w_own, w_other, *got)


def out_weight_kernel(n, place_ref, *refs):
    mixed_refs, mid_ref, out_ref = refs[:n], refs[n], refs[-1]
    for s in range(n):
        t = lax.rem(place_ref[0] - s + n, n)
        grad = mm_tn(mixed_refs[s][...], mid_ref[...])
        if len(refs) > n + 2:
            grad = grad + refs[n + 1][0, t].astype(F32)
        out_ref[0, t] = grad.astype(BF16)


def out_weight_grad(place, side, mixed, mid, n, chips, got):
    rows, width = mid.shape
    cols = mixed[0].shape[1]
    own = width // (2 * chips)
    block = pl.BlockSpec((1, n, cols, own), lambda c, place: (c, 0, 0, 0))
    extra = [] if got is None else [got]
    return call(
        functools.partial(out_weight_kernel, n),
        pltpu.PrefetchScalarGridSpec(
            num_scalar_prefetch=1,
            grid=(chips,),
            in_specs=[pl.BlockSpec((rows, cols), lambda c, place: (0, 0))] * n
            + [pl.BlockSpec((rows, own), lambda c, place: (0, 2 * c + place[3]))]
            + [block] * len(extra),
            out_specs=block,
        ),
        shape((chips, n, cols, own), BF16),
        rows * width * cols * n,
        n * cols * width,
    )(jnp.concatenate([place, side]), *mixed, mid, *extra)


def entry_kernel(sid_ref, grad_ref, w_ref, out_ref):
    out_ref[...] = mm_nt(grad_ref[...], w_ref[...]).astype(BF16)


def entry_shard(sid, grads, w_qkv, rows):
    width, cols = w_qkv.shape
    tile = width // 4
    return call(
        entry_kernel,
        pltpu.PrefetchScalarGridSpec(
            num_scalar_prefetch=1,
            grid=(4,),
            in_specs=[
                pl.BlockSpec((rows, cols), lambda j, sid: (sid[0], 0)),
                pl.BlockSpec((tile, cols), lambda j, sid: (j, 0)),
            ],
            out_specs=pl.BlockSpec((rows, tile), lambda j, sid: (0, j)),
        ),
        shape((rows, width), BF16),
        2 * rows * width * cols,
        2 * (width * cols + rows * cols + rows * width),
    )(sid, grads, w_qkv)


def rows_grad_kernel(x_ref, gate_ref, up_ref, out_ref):
    units = gate_ref.shape[1]
    for j, ref in enumerate((gate_ref, up_ref)):
        out_ref[0, :, j * units : (j + 1) * units] = mm_tn(x_ref[...], ref[...]).astype(BF16)


def gate_up_grad(x, gate_grad, up_grad, batches):
    block_rows, width = x.shape
    units = gate_grad.shape[1]
    rows = width // batches
    whole = lambda j: (0, 0)
    return call(
        rows_grad_kernel,
        pltpu.PrefetchScalarGridSpec(
            num_scalar_prefetch=0,
            grid=(batches,),
            in_specs=[
                pl.BlockSpec((block_rows, rows), lambda j: (0, j)),
                pl.BlockSpec((block_rows, units), whole),
                pl.BlockSpec((block_rows, units), whole),
            ],
            out_specs=pl.BlockSpec((1, rows, 2 * units), lambda j: (j, 0, 0)),
        ),
        shape((batches, rows, 2 * units), BF16),
        4 * block_rows * width * units,
        2 * (block_rows * width + 2 * block_rows * units + 2 * width * units),
    )(x, gate_grad, up_grad)


def cols_grad_kernel(active_ref, grad_ref, out_ref):
    out_ref[0] = mm_tn(active_ref[...], grad_ref[...]).astype(BF16)


def down_grad(active, grad_all, batches):
    block_rows, units = active.shape
    width = grad_all.shape[1]
    cols = width // batches
    return call(
        cols_grad_kernel,
        pltpu.PrefetchScalarGridSpec(
            num_scalar_prefetch=0,
            grid=(batches,),
            in_specs=[
                pl.BlockSpec((block_rows, units), lambda j: (0, 0)),
                pl.BlockSpec((block_rows, cols), lambda j: (0, j)),
            ],
            out_specs=pl.BlockSpec((1, units, cols), lambda j: (j, 0, 0)),
        ),
        shape((batches, units, cols), BF16),
        2 * block_rows * width * units,
        2 * (block_rows * units + block_rows * width + width * units),
    )(active, grad_all)


def qkv_weight_kernel(side_ref, entry_ref, grad_ref, w_ref, out_ref, part_ref):
    grad = mm_tn(entry_ref[...], grad_ref[...])
    out_ref[0] = grad.astype(BF16)
    both = grad * w_ref[...].astype(F32)
    lanes = part_ref.shape[2]
    total = both[:, :lanes]
    for first in range(lanes, both.shape[1], lanes):
        total = total + both[:, first : first + lanes]
    part_ref[0] = total


def qkv_weight_grad(side, entry, grads, w_qkv, chips):
    block_rows, width = entry.shape
    cols = grads.shape[1]
    rows = width // (2 * chips)
    return call(
        qkv_weight_kernel,
        pltpu.PrefetchScalarGridSpec(
            num_scalar_prefetch=1,
            grid=(chips,),
            in_specs=[
                pl.BlockSpec((block_rows, rows), lambda j, side: (0, 2 * j + side[0])),
                pl.BlockSpec((block_rows, cols), lambda j, side: (0, 0)),
                pl.BlockSpec((rows, cols), lambda j, side: (2 * j + side[0], 0)),
            ],
            out_specs=[
                pl.BlockSpec((1, rows, cols), lambda j, side: (j, 0, 0)),
                pl.BlockSpec((1, rows, 128), lambda j, side: (j, 0, 0)),
            ],
        ),
        [shape((chips, rows, cols), BF16), shape((chips, rows, 128), F32)],
        block_rows * width * cols,
        2 * (block_rows * width + block_rows * cols + 2 * width * cols),
    )(side, entry, grads, w_qkv)


def exchange(value, axis, step):
    size = lax.axis_size(axis)
    return lax.ppermute(value, axis, [(i, i ^ step) for i in range(size)])


def total_over(value, axis):
    step = 1
    while step < lax.axis_size(axis):
        value = value + exchange(value, axis, step)
        step *= 2
    return value


@jax.tree_util.register_pytree_node_class
class Halves:
    def __init__(self, values, axes):
        self.values, self.axes = tuple(values), tuple(axes)

    def tree_flatten(self):
        return self.values, self.axes

    @classmethod
    def tree_unflatten(cls, axes, values):
        return cls(values, axes)

    def orders(self, batches):
        bits = tuple(range(1, batches.bit_length() - 1))
        return bits, bits[::-1]

    def send(self, step, batches):
        done = [send_half(v, a, o[step]) for v, a, o in zip(self.values, self.axes, self.orders(batches))]
        kept, got, axes = zip(*done)
        return Halves(kept, axes), got

    def add(self, got):
        values = [v.astype(F32) + g.astype(F32) for v, g in zip(self.values, got)]
        return Halves(values, self.axes)

    def double(self, step, batches):
        done = []
        for value, axes, order in zip(self.values, self.axes, self.orders(batches)):
            got = exchange(value, DP, 1 << order[step])
            done.append((jnp.stack([value, got]), (order[step],) + axes))
        return Halves(*zip(*done))

    def pieces(self, batches):
        bits = self.orders(batches)[1]
        done = []
        for value, axes in zip(self.values, self.axes):
            rest = list(range(len(axes), value.ndim))
            value = value.transpose([axes.index(bit) for bit in bits] + rest)
            done.append(value.reshape((batches // 2,) + value.shape[len(axes) :]))
        return jnp.concatenate(done, axis=2)


def send_half(value, axes, bit):
    own = lax.rem(lax.div(lax.axis_index(DP), 1 << bit), 2)
    at = axes.index(bit)
    sent = lax.dynamic_index_in_dim(value, 1 - own, at, False).astype(BF16)
    kept = lax.dynamic_index_in_dim(value, own, at, False)
    return kept, exchange(sent, DP, 1 << bit), axes[:at] + axes[at + 1 :]


def halves_of(value):
    bits = value.shape[0].bit_length() - 1
    value = value.reshape((2,) * bits + value.shape[1:])
    axes = tuple(range(1, bits + 1))[::-1]
    middle = value.shape[-1] // 2
    return Halves((value[..., :middle], value[..., middle:]), (axes, axes))


def join(*values):
    return lax.optimization_barrier(values)


def add_low(a, b):
    return (a.astype(F32) + b.astype(F32)).astype(BF16)


class RingSum:
    def __init__(self, shift):
        self.parts, self.shift, self.step, self.moving = [], shift, 0, None

    def add(self):
        self.step += 1
        if self.step < len(self.parts):
            part = self.parts[self.step]
            self.moving = part if self.step == 1 else add_low(self.moving, part)

    def send(self):
        if self.step < len(self.parts):
            self.moving = self.shift(self.moving)

    def hop(self):
        self.add()
        self.send()


def total_of(own, got):
    total = own.astype(F32)
    for value in got:
        total = total + value.astype(F32)
    return total


def local(
    tokens,
    seq_lengths,
    attn_gain,
    mlp_gain,
    q_gain,
    k_gain,
    w_query,
    key_weight,
    value_weight,
    w_out,
    w_gate,
    w_up,
    w_down,
    out_grad,
):
    n = lax.axis_size("tensor")
    batches = lax.axis_size(DP)
    rows, width = tokens.shape
    block_rows = rows * n
    dim = q_gain.shape[0]
    heads = w_query.shape[1] // dim
    kv_heads = key_weight.shape[1] // dim
    z = lax.axis_index("tensor").astype(jnp.int32)
    zs = z.reshape(1)
    ring = [(i, (i + 1) % n) for i in range(n)]
    shift = lambda v, d=1: lax.ppermute(v, "tensor", [(i, (i + d) % n) for i in range(n)])
    shard_of = lambda s: lax.rem(z - s + n, n).reshape(1)

    chips = batches // 2
    core = lax.axis_index("core").astype(jnp.int32).reshape(1)
    place = jnp.stack([z, lax.axis_index("chip").astype(jnp.int32), core[0]])
    steps = batches.bit_length() - 2

    own_cols = width // batches
    piece = lax.dynamic_slice_in_dim(w_out, lax.axis_index(DP) * own_cols, own_cols, 1)
    piece = lax.all_gather(piece, "tensor", axis=0, tiled=False)

    offset, position = positions_of(seq_lengths[0], block_rows)
    start = offset[None, :]
    cosine, sine = rope_tables(position, dim)
    w_qkv = jnp.concatenate([w_query, key_weight, value_weight], axis=1)
    gain_one, gain_two = attn_gain[None, :], mlp_gain[None, :]
    qg, kg = q_gain[None, :], k_gain[None, :]

    came = shift(tokens)
    came, piece, w_qkv, cosine, sine, start = join(came, piece, w_qkv, cosine, sine, start)
    blocks = [tokens, came]
    middle = piece.shape[1] // 2
    halves = Halves((piece[:, :middle], piece[:, middle:]), ((), ()))
    kept, ready = None, 0
    for s in range(1, n):
        came = shift(blocks[s]) if s < n - 1 else None
        while ready <= s:
            kept = qkv_shard(
                shard_of(ready), blocks[ready], gain_one, w_qkv, cosine, sine, qg, kg, heads, kv_heads,
                dim, block_rows, kept,
            )
            ready += 1
        if s <= steps:
            halves = halves.double(s - 1, batches)
        if came is not None:
            came, kept, halves = join(came, kept, halves)
            blocks.append(came)
    entry_all, side, raw = kept
    w_own = halves.pieces(batches)
    w_other = exchange(w_own, "core", 1)

    later_grad, _ = join(out_grad, blocks[-1])
    grad_all = lax.all_gather(later_grad, "tensor", axis=0, tiled=True)

    mixed, lse = attention_forward(zs, side, start, n, heads, kv_heads, dim)
    mixed, w_own = join(mixed, w_own)
    mixed = [mixed[0]] + [shift(mixed[d], d) for d in range(1, n)]
    mixed, w_other = join(mixed, w_other)
    hidden, mlp_entry = out_projection(place, mixed, w_own, w_other, tokens, gain_two, n)

    weights = (w_gate, w_up, w_down)
    down_sum, inner_sum = RingSum(shift), RingSum(shift)
    over_dp = lambda g: lax.psum_scatter(g, DP, scatter_dimension=0, tiled=False)
    blocks, kept = [mlp_entry], None
    for t in range(2 * n - 2):
        if t < n - 1:
            blocks.append(shift(blocks[t]))
        else:
            inner_sum.hop()
        for s in {0: (0,), 1: (), 2: (1, 2)}.get(t, (t,)):
            if s < n:
                kept, down, inner = mlp_shard(
                    shard_of(s), blocks[s], grad_all if s else out_grad, weights, kept, block_rows
                )
                down_sum.parts.append(down)
                inner_sum.parts.append(inner)
        if t == 1:
            blocks, kept, grad_all = join(blocks, kept, grad_all)
        elif t == 2 * n - 4:
            w_down_grad = down_grad(active, grad_all, batches)
            inner_sum.moving, w_down_grad = join(inner_sum.moving, w_down_grad)
            w_down_grad = over_dp(w_down_grad)
        elif t == 2 * n - 3:
            down_sum.hop()
            w_gate_up_grad = gate_up_grad(mlp_all, gate_grad, up_grad, batches)
            inner_sum.moving, down_sum.moving, w_gate_up_grad = join(
                inner_sum.moving, down_sum.moving, w_gate_up_grad
            )
            w_gate_up_grad = over_dp(w_gate_up_grad)
        else:
            blocks, kept, inner_sum.parts, inner_sum.moving = join(
                blocks, kept, inner_sum.parts, inner_sum.moving
            )
            active, gate_grad, up_grad, mlp_all = kept

    gm, grad_hidden, grad_mid, mlp_part = mid_stage(
        place, inner_sum.parts[0], (inner_sum.moving,), out_grad, hidden, gain_two, w_own, w_other, n
    )

    gm = [gm[0]] + [shift(gm[d], d) for d in range(1, n)]
    got = out_weight_grad(place, 1 - core, mixed, grad_mid, n, chips, None)
    down_sum.add()
    gm, got, down_sum.moving = join(gm, got, down_sum.moving)

    down_sum.send()
    got = exchange(got, "core", 1)
    grads, gain_parts = attention_backward(
        zs, gm, side, raw, lse, start, cosine, sine, qg, kg, heads, kv_heads, dim
    )

    entry_part = lambda s: entry_shard(shard_of(s), grads, w_qkv, rows)
    entry_sum = RingSum(shift)
    entry_sum.parts = [None, entry_part(1)] + [None] * (n - 2)
    w_out_grad = out_weight_grad(place, core, mixed, grad_mid, n, chips, got)
    entry_sum.parts[1], grads, w_out_grad, down_sum.moving = join(
        entry_sum.parts[1], grads, w_out_grad, down_sum.moving
    )

    down_sum.add()
    out_halves = halves_of(w_out_grad)
    entry_sum.add()

    entry_sum.send()
    down_sum.send()
    out_halves, out_got = out_halves.send(0, batches)
    qkv_sent, lanes_sent = qkv_weight_grad(1 - core, entry_all, grads, w_qkv, chips)
    w_qkv_grad, lanes = qkv_weight_grad(core, entry_all, grads, w_qkv, chips)
    entry_sum.parts[2 % n] = entry_part(2 % n)
    entry_sum.add()
    state = (entry_sum.moving, down_sum.moving, out_halves, out_got, qkv_sent, w_qkv_grad)
    state, grads, lanes, lanes_sent = join(state, grads, lanes, lanes_sent)
    entry_sum.moving, down_sum.moving, out_halves, out_got, qkv_sent, w_qkv_grad = state
    lanes, lanes_sent = jnp.sum(lanes, axis=2), jnp.sum(lanes_sent, axis=2)
    lanes = jnp.where(core[0] == 0, jnp.stack([lanes, lanes_sent], 1), jnp.stack([lanes_sent, lanes], 1))
    attn_part = lanes.reshape(width) / attn_gain
    totals = jnp.concatenate([attn_part, mlp_part[0], gain_parts[0], gain_parts[1]])[None, :]

    entry_sum.send()
    down_sum.add()
    down_sum.send()
    out_halves = out_halves.add(out_got)
    if steps > 1:
        out_halves, out_got = out_halves.send(1, batches)
    qkv_got = exchange(qkv_sent, "core", 1)
    totals = total_over(totals, "tensor")
    entry_sum.parts[3 % n] = entry_part(3 % n)
    entry_sum.add()
    state = (entry_sum.moving, down_sum.moving, out_halves, out_got, qkv_got, w_qkv_grad)
    state, grads, totals = join(state, grads, totals)
    entry_sum.moving, down_sum.moving, out_halves, out_got, qkv_got, w_qkv_grad = state

    if steps > 1:
        out_halves = out_halves.add(out_got)
    for step in range(2, steps):
        out_halves, out_got = out_halves.send(step, batches)
        out_halves = out_halves.add(out_got)
    w_out_grad = jnp.concatenate(out_halves.values, axis=-1).astype(BF16)
    out_sum = RingSum(shift)
    out_sum.parts = [lax.dynamic_index_in_dim(w_out_grad, shard_of(d)[0], 0, False) for d in range(n)]
    for _ in range(n - 1):
        out_sum.hop()
    qkv_halves = halves_of(add_low(w_qkv_grad, qkv_got))
    for step in range(steps):
        qkv_halves, qkv_got = qkv_halves.send(step, batches)
        if step < steps - 1:
            qkv_halves = qkv_halves.add(qkv_got)
    totals = total_over(totals, DP)
    for s in range(3, n):
        entry_sum.send()
        down_sum.add()
        down_sum.send()
        entry_sum.parts[(s + 1) % n] = entry_part((s + 1) % n)
        if s < n - 1:
            entry_sum.add()
            entry_sum.moving, down_sum.moving, grads = join(entry_sum.moving, down_sum.moving, grads)
    grad_entry = total_of(entry_sum.parts[0], [entry_sum.moving]).astype(F32)
    state = (grad_entry, qkv_halves, qkv_got, out_sum.parts[0], out_sum.moving)
    (grad_entry, qkv_halves, qkv_got, own, moved), w_down_grad, w_gate_up_grad, totals = join(
        state, w_down_grad, w_gate_up_grad, totals
    )
    w_out_grad = total_of(own, [moved])
    w_qkv_grad = jnp.concatenate(qkv_halves.add(qkv_got).values, axis=-1)
    output = total_of(hidden, [down_sum.parts[0], down_sum.moving]).astype(BF16)

    x = tokens.astype(F32)
    scale = inv_root_of(x)
    token_grad = (grad_hidden + norm_back(grad_entry * attn_gain, x * scale, scale)).astype(BF16)

    totals = totals[0]
    attn_gain_grad = totals[:width]
    mlp_gain_grad = totals[width : 2 * width]
    q_gain_grad = totals[2 * width : 2 * width + dim]
    k_gain_grad = totals[2 * width + dim :]
    w_down_grad, w_gate_up_grad = w_down_grad.astype(F32), w_gate_up_grad.astype(F32)
    a, b = heads * dim, (heads + kv_heads) * dim
    return (
        output,
        token_grad,
        attn_gain_grad,
        mlp_gain_grad,
        q_gain_grad,
        k_gain_grad,
        w_qkv_grad[:, :a],
        w_qkv_grad[:, a:b],
        w_qkv_grad[:, b:],
        w_out_grad,
        w_gate_up_grad[:, : w_gate.shape[1]],
        w_gate_up_grad[:, w_gate.shape[1] :],
        w_down_grad,
    )


def solution(mesh):
    batches, shards = mesh.shape["dp"], mesh.shape["tensor"]
    return jax.shard_map(
        local,
        mesh=Mesh(mesh.devices.reshape(batches // 2, 2, shards), DP + ("tensor",)),
        in_specs=(
            P(("chip", "core", "tensor"), None),
            P(DP, None),
            P(),
            P(),
            P(),
            P(),
            P(None, "tensor"),
            P(None, "tensor"),
            P(None, "tensor"),
            P("tensor", None),
            P(None, "tensor"),
            P(None, "tensor"),
            P("tensor", None),
            P(("chip", "core", "tensor"), None),
        ),
        out_specs=(
            P(("chip", "core", "tensor"), None),
            P(("chip", "core", "tensor"), None),
            P(),
            P(),
            P(),
            P(),
            P(DP, "tensor"),
            P(DP, "tensor"),
            P(DP, "tensor"),
            P("tensor", DP),
            P(DP, "tensor"),
            P(DP, "tensor"),
            P("tensor", DP),
        ),
        check_vma=False,
    )
```

```python
import functools

import jax
import jax.numpy as jnp
from jax import lax
from jax.experimental import pallas as pl
from jax.experimental.pallas import tpu as pltpu
from jax.sharding import Mesh, PartitionSpec as P

NORM_EPSILON = 1e-06
ROPE_BASE = 1000000.0
MASK_FILL = -1e30
VMEM_BYTES = 52 * 1024 * 1024
F32 = jnp.float32
BF16 = jnp.bfloat16
DP = ("chip", "core")
COST = 1000

NT = (((1,), (1,)), ((), ()))
TN = (((0,), (0,)), ((), ()))


def mm(a, b):
    return jnp.dot(a, b, preferred_element_type=F32)


def mm_nt(a, b):
    return lax.dot_general(a, b, NT, preferred_element_type=F32)


def mm_tn(a, b):
    return lax.dot_general(a, b, TN, preferred_element_type=F32)


def inv_root_of(values):
    return lax.rsqrt(jnp.mean(values * values, axis=-1, keepdims=True) + NORM_EPSILON)


def norm_back(grad_normed, normal, inv_root):
    return inv_root * (
        grad_normed - normal * jnp.mean(grad_normed * normal, axis=-1, keepdims=True)
    )


def call(kernel, grid_spec, out_shape, flops, nbytes, aliases=None):
    return pl.pallas_call(
        kernel,
        grid_spec=grid_spec,
        out_shape=out_shape,
        input_output_aliases=aliases or {},
        compiler_params=pltpu.CompilerParams(vmem_limit_bytes=VMEM_BYTES),
        cost_estimate=pl.CostEstimate(flops=flops // COST, bytes_accessed=nbytes // COST, transcendentals=0),
    )


def shape(dims, dtype):
    return jax.ShapeDtypeStruct(dims, dtype)


def positions_of(lengths, count_of_rows):
    seq_ends = jnp.cumsum(lengths, dtype=jnp.int32)
    starts = seq_ends - lengths
    place_index = jnp.arange(count_of_rows, dtype=jnp.int32)
    segment = jnp.sum(
        (place_index[:, None] >= seq_ends[None, :]).astype(jnp.int32), axis=1, dtype=jnp.int32
    )
    belongs = segment[:, None] == jnp.arange(lengths.shape[0], dtype=jnp.int32)[None, :]
    offset = jnp.sum(jnp.where(belongs, starts[None, :], 0), axis=1, dtype=jnp.int32)
    return (offset, place_index - offset)


def rope_tables(position, head_width):
    half_width = head_width // 2
    frequency = ROPE_BASE ** (-2.0 * jnp.arange(half_width, dtype=F32) / head_width)
    angles = position.astype(F32)[:, None] * frequency[None, :]
    cosine, sine = jnp.cos(angles), jnp.sin(angles)
    return (
        jnp.concatenate([cosine, cosine], axis=1),
        jnp.concatenate([-sine, sine], axis=1),
    )


def qkv_kernel(heads, kv_heads, dim, sid_ref, x_ref, gain_ref, w_ref, cos_ref, sin_ref, qg_ref, kg_ref, *refs):
    entry_ref, side_ref, raw_ref = refs[-3:]
    x = x_ref[...].astype(F32)
    entry = (x * inv_root_of(x) * gain_ref[...]).astype(BF16)
    entry_ref[...] = entry
    both = mm(entry, w_ref[...])
    cosine, sine = cos_ref[...], sin_ref[...]
    for h in range(heads + kv_heads):
        cols = slice(h * dim, (h + 1) * dim)
        raw = both[:, cols]
        raw_ref[:, cols] = raw.astype(BF16)
        gain = qg_ref[...] if h < heads else kg_ref[...]
        u = raw * inv_root_of(raw) * gain
        turned = u * cosine + pltpu.roll(u, dim // 2, 1) * sine
        if h < heads:
            turned = turned * dim ** (-0.5)
        side_ref[:, cols] = turned.astype(BF16)
    rest = slice((heads + kv_heads) * dim, (heads + 2 * kv_heads) * dim)
    side_ref[:, rest] = both[:, rest].astype(BF16)


def qkv_shard(sid, x, gain, w_qkv, cosine, sine, q_gain, k_gain, heads, kv_heads, dim, block_rows, kept):
    rows, width = x.shape
    cols = w_qkv.shape[1]
    raw_cols = (heads + kv_heads) * dim
    whole = lambda i, sid: (0, 0)
    mine = lambda i, sid: (sid[0], 0)
    in_specs = [
        pl.BlockSpec((rows, width), whole),
        pl.BlockSpec((1, width), whole),
        pl.BlockSpec((width, cols), whole),
        pl.BlockSpec((rows, dim), mine),
        pl.BlockSpec((rows, dim), mine),
        pl.BlockSpec((1, dim), whole),
        pl.BlockSpec((1, dim), whole),
    ]
    args = [sid, x, gain, w_qkv, cosine, sine, q_gain, k_gain]
    aliases = {}
    if kept is not None:
        for j, array in enumerate(kept):
            aliases[len(args)] = j
            args.append(array)
            in_specs.append(pl.BlockSpec(memory_space=pl.ANY))
    return call(
        functools.partial(qkv_kernel, heads, kv_heads, dim),
        pltpu.PrefetchScalarGridSpec(
            num_scalar_prefetch=1,
            grid=(1,),
            in_specs=in_specs,
            out_specs=[
                pl.BlockSpec((rows, width), mine),
                pl.BlockSpec((rows, cols), mine),
                pl.BlockSpec((rows, raw_cols), mine),
            ],
        ),
        [
            shape((block_rows, width), BF16),
            shape((block_rows, cols), BF16),
            shape((block_rows, raw_cols), BF16),
        ],
        2 * rows * width * cols,
        2 * (2 * rows * width + width * cols + 2 * rows * cols),
        aliases,
    )(*args)


def visible_keys(start_ref, first_row, rows, keys):
    key = lax.broadcasted_iota(jnp.int32, (keys, rows), 0)
    query = first_row + lax.broadcasted_iota(jnp.int32, (keys, rows), 1)
    return (key <= query) & (key >= start_ref[:, first_row : first_row + rows])


def attention_kernel(n, heads, kv_heads, dim, z_ref, side_ref, start_ref, mixed_ref, lse_ref):
    rows = side_ref.shape[0] // n
    group = heads // kv_heads
    for i in range(n):
        slot = lax.rem(i - z_ref[0] + n, n)
        keys = (i + 1) * rows
        here = slice(i * rows, (i + 1) * rows)
        visible = visible_keys(start_ref, i * rows, rows, keys)
        for h in range(heads):
            kv = h // group
            key = side_ref[:keys, (heads + kv) * dim : (heads + kv + 1) * dim]
            value = side_ref[
                :keys, (heads + kv_heads + kv) * dim : (heads + kv_heads + kv + 1) * dim
            ]
            cols = slice(h * dim, (h + 1) * dim)
            scores = jnp.where(visible, mm_nt(key, side_ref[here, cols]), MASK_FILL)
            peak = jnp.max(scores, axis=0, keepdims=True)
            spread = jnp.exp(scores - peak)
            total = jnp.sum(spread, axis=0, keepdims=True)
            mixed = mm_tn(value, spread.astype(BF16)) / total
            mixed_ref[slot, :, cols] = mixed.T.astype(BF16)
            lse_ref[h : h + 1, here] = peak + jnp.log(total)


def attention_forward(z, side, start, n, heads, kv_heads, dim):
    block_rows = side.shape[0]
    rows = block_rows // n
    whole2 = lambda i, z: (0, 0)
    return call(
        functools.partial(attention_kernel, n, heads, kv_heads, dim),
        pltpu.PrefetchScalarGridSpec(
            num_scalar_prefetch=1,
            grid=(1,),
            in_specs=[
                pl.BlockSpec(side.shape, whole2),
                pl.BlockSpec((1, block_rows), whole2),
            ],
            out_specs=[
                pl.BlockSpec((n, rows, heads * dim), lambda i, z: (0, 0, 0)),
                pl.BlockSpec((heads, block_rows), whole2),
            ],
        ),
        [shape((n, rows, heads * dim), BF16), shape((heads, block_rows), F32)],
        2 * block_rows * block_rows * heads * dim * 2,
        2 * side.size + 6 * block_rows * heads * dim,
    )(z, side, start)


def attention_back_kernel(n, heads, kv_heads, dim, z_ref, *refs):
    gm_refs = refs[:n]
    side_ref, raw_ref, lse_ref, start_ref, cos_ref, sin_ref, qg_ref, kg_ref = refs[n : n + 8]
    out_ref, gain_ref, gm_ref, key_acc, value_acc = refs[n + 8 :]
    block_rows = side_ref.shape[0]
    rows = block_rows // n
    group = heads // kv_heads
    q_sum = jnp.zeros((1, dim), F32)
    k_sum = jnp.zeros((1, dim), F32)
    for slot, ref in enumerate(gm_refs):
        gm_ref[slot] = ref[...]
    for kv in range(kv_heads):
        key_cols = slice((heads + kv) * dim, (heads + kv + 1) * dim)
        value_cols = slice((heads + kv_heads + kv) * dim, (heads + kv_heads + kv + 1) * dim)
        key_acc[...] = jnp.zeros_like(key_acc)
        value_acc[...] = jnp.zeros_like(value_acc)
        for i in range(n):
            slot = lax.rem(z_ref[0] - i + n, n)
            keys = (i + 1) * rows
            here = slice(i * rows, (i + 1) * rows)
            key = side_ref[:keys, key_cols]
            value = side_ref[:keys, value_cols]
            visible = visible_keys(start_ref, i * rows, rows, keys)
            cosine, sine = cos_ref[here, :], sin_ref[here, :]
            for g in range(group):
                h = kv * group + g
                cols = slice(h * dim, (h + 1) * dim)
                query = side_ref[here, cols]
                grad = gm_ref[slot, :, cols]
                scores = jnp.where(visible, mm_nt(key, query), MASK_FILL)
                soft = jnp.exp(scores - lse_ref[h : h + 1, here])
                grad_weights = mm_nt(value, grad)
                inner = jnp.sum(soft * grad_weights, axis=0, keepdims=True)
                grad_scores = (soft * (grad_weights - inner)).astype(BF16)
                value_acc[:keys, :] += mm(soft.astype(BF16), grad)
                key_acc[:keys, :] += mm(grad_scores, query)
                turned = mm_tn(key, grad_scores).T * dim ** (-0.5)
                back = turned * cosine - pltpu.roll(turned, dim // 2, 1) * sine
                raw = raw_ref[here, cols].astype(F32)
                scale = inv_root_of(raw)
                normal = raw * scale
                q_sum = q_sum + jnp.sum(back * normal, axis=0, keepdims=True)
                out_ref[here, cols] = norm_back(back * qg_ref[...], normal, scale).astype(BF16)
        turned = key_acc[...]
        back = turned * cos_ref[...] - pltpu.roll(turned, dim // 2, 1) * sin_ref[...]
        raw = raw_ref[:, key_cols].astype(F32)
        scale = inv_root_of(raw)
        normal = raw * scale
        k_sum = k_sum + jnp.sum(back * normal, axis=0, keepdims=True)
        out_ref[:, key_cols] = norm_back(back * kg_ref[...], normal, scale).astype(BF16)
        out_ref[:, value_cols] = value_acc[...].astype(BF16)
    gain_ref[...] = jnp.concatenate([q_sum, k_sum, jnp.zeros((6, dim), F32)], axis=0)


def attention_backward(z, gm, side, raw, lse, start, cosine, sine, q_gain, k_gain, heads, kv_heads, dim):
    n = len(gm)
    block_rows = side.shape[0]
    whole2 = lambda i, z: (0, 0)
    ins = (*gm, side, raw, lse, start, cosine, sine, q_gain, k_gain)
    return call(
        functools.partial(attention_back_kernel, n, heads, kv_heads, dim),
        pltpu.PrefetchScalarGridSpec(
            num_scalar_prefetch=1,
            grid=(1,),
            in_specs=[pl.BlockSpec(a.shape, whole2) for a in ins],
            out_specs=[pl.BlockSpec(side.shape, whole2), pl.BlockSpec((8, dim), whole2)],
            scratch_shapes=[
                pltpu.VMEM((n,) + gm[0].shape, BF16),
                pltpu.VMEM((block_rows, dim), F32),
                pltpu.VMEM((block_rows, dim), F32),
            ],
        ),
        [shape(side.shape, BF16), shape((8, dim), F32)],
        2 * block_rows * block_rows * heads * dim * 5,
        12 * side.size,
    )(z, *ins)


def column_block(place_ref, k, other, cols):
    block = 2 * lax.bitwise_xor(place_ref[1], k) + (1 - place_ref[2] if other else place_ref[2])
    return pl.ds(pl.multiple_of(block * cols, cols), cols)


def out_kernel(n, chips, place_ref, *refs):
    mixed_refs = refs[:n]
    own_ref, other_ref, x_ref, gain_ref, hidden_ref, entry_ref, acc = refs[n:]
    k = pl.program_id(0)
    for other, w_ref in enumerate((own_ref, other_ref)):
        part = mm(mixed_refs[0][...], w_ref[0, place_ref[0]])
        for s in range(1, n):
            part = part + mm(mixed_refs[s][...], w_ref[0, lax.rem(place_ref[0] - s + n, n)])
        acc[:, column_block(place_ref, k, other, part.shape[1])] = part

    @pl.when(k == chips - 1)
    def _():
        hidden = acc[...] + x_ref[...].astype(F32)
        hidden_ref[...] = hidden
        entry_ref[...] = (hidden * inv_root_of(hidden) * gain_ref[...]).astype(BF16)


def out_projection(place, mixed, w_own, w_other, x, gain, n):
    rows, width = x.shape
    chips = w_own.shape[0]
    whole = lambda k, place: (0, 0)
    block = pl.BlockSpec((1,) + w_own.shape[1:], lambda k, place: (k, 0, 0, 0))
    return call(
        functools.partial(out_kernel, n, chips),
        pltpu.PrefetchScalarGridSpec(
            num_scalar_prefetch=1,
            grid=(chips,),
            in_specs=[pl.BlockSpec(mixed[0].shape, whole)] * n
            + [
                block,
                block,
                pl.BlockSpec((rows, width), whole),
                pl.BlockSpec((1, width), whole),
            ],
            out_specs=[pl.BlockSpec((rows, width), whole), pl.BlockSpec((rows, width), whole)],
            scratch_shapes=[pltpu.VMEM((rows, width), F32)],
        ),
        [shape((rows, width), F32), shape((rows, width), BF16)],
        4 * rows * w_own.size,
        4 * w_own.size + 10 * rows * width,
    )(place, *mixed, w_own, w_other, x, gain)


def mlp_kernel(tiles, sid_ref, x_ref, go_ref, wg_ref, wu_ref, wd_ref, *refs):
    active_ref, gate_grad_ref, up_grad_ref, copy_ref, down_ref, inner_ref, down_acc, inner_acc = refs[-8:]
    j = pl.program_id(0)
    x = x_ref[...]
    gate = mm(x, wg_ref[...])
    up = mm(x, wu_ref[...])
    sigmoid = jax.nn.sigmoid(gate)
    silu = gate * sigmoid
    active = (silu * up).astype(BF16)
    active_ref[...] = active
    grad_active = mm_nt(go_ref[...], wd_ref[...])
    gate_grad = (grad_active * up * sigmoid * (1.0 + gate * (1.0 - sigmoid))).astype(BF16)
    up_grad = (grad_active * silu).astype(BF16)
    gate_grad_ref[...] = gate_grad
    up_grad_ref[...] = up_grad
    inner = mm_nt(gate_grad, wg_ref[...]) + mm_nt(up_grad, wu_ref[...])
    down = mm(active, wd_ref[...])

    @pl.when(j == 0)
    def _():
        copy_ref[...] = x
        inner_acc[...] = inner
        down_acc[...] = down

    @pl.when(j > 0)
    def _():
        inner_acc[...] += inner
        down_acc[...] += down

    @pl.when(j == tiles - 1)
    def _():
        inner_ref[...] = inner_acc[...].astype(BF16)
        down_ref[...] = down_acc[...].astype(BF16)


def mlp_shard(sid, x, grads, weights, kept, block_rows):
    w_gate, w_up, w_down = weights
    rows, width = x.shape
    units = w_gate.shape[1]
    tile = next(t for t in (512, 384, 256, 128) if units % t == 0)
    tiles = units // tile
    whole = pl.BlockSpec((rows, width), lambda j, sid: (0, 0))
    mine = pl.BlockSpec((rows, width), lambda j, sid: (sid[0], 0))
    tiled = pl.BlockSpec((rows, tile), lambda j, sid: (sid[0], j))
    column = pl.BlockSpec((width, tile), lambda j, sid: (0, j))
    in_specs = [
        whole,
        whole if grads.shape[0] == rows else mine,
        column,
        column,
        pl.BlockSpec((tile, width), lambda j, sid: (j, 0)),
    ]
    args = [sid.reshape(1), x, grads, w_gate, w_up, w_down]
    aliases = {}
    if kept is not None:
        for j, array in enumerate(kept):
            aliases[len(args)] = j
            args.append(array)
            in_specs.append(pl.BlockSpec(memory_space=pl.ANY))
    *kept, down, inner = call(
        functools.partial(mlp_kernel, tiles),
        pltpu.PrefetchScalarGridSpec(
            num_scalar_prefetch=1,
            grid=(tiles,),
            in_specs=in_specs,
            out_specs=[tiled] * 3 + [mine] + [whole] * 2,
            scratch_shapes=[pltpu.VMEM((rows, width), F32), pltpu.VMEM((rows, width), F32)],
        ),
        [shape((block_rows, units), BF16)] * 3
        + [shape((block_rows, width), BF16)]
        + [shape((rows, width), BF16)] * 2,
        2 * rows * width * units * 6,
        2 * (3 * width * units + 3 * rows * units + 5 * rows * width),
        aliases,
    )(*args)
    return kept, down, inner


def mid_kernel(n, chips, place_ref, own_part_ref, go_ref, hidden_ref, gain_ref, own_ref, other_ref, *refs):
    got_refs = refs[:-5]
    gm_ref, gh_ref, mid_ref, part_ref, acc = refs[-5:]
    k = pl.program_id(0)

    @pl.when(k == 0)
    def _():
        hidden = hidden_ref[...]
        scale = inv_root_of(hidden)
        normal = hidden * scale
        inner = own_part_ref[...].astype(F32)
        for ref in got_refs:
            inner = inner + ref[...].astype(F32)
        part_ref[...] = jnp.sum(inner * normal, axis=0, keepdims=True)
        grad_hidden = go_ref[...].astype(F32) + norm_back(inner * gain_ref[...], normal, scale)
        gh_ref[...] = grad_hidden
        mid_ref[...] = grad_hidden.astype(BF16)
        acc[...] = jnp.zeros_like(acc)

    cols = own_ref.shape[3]
    own = mid_ref[:, column_block(place_ref, k, False, cols)]
    other = mid_ref[:, column_block(place_ref, k, True, cols)]
    for s in range(n):
        t = lax.rem(place_ref[0] + s, n)
        acc[s] += mm_nt(own, own_ref[0, t]) + mm_nt(other, other_ref[0, t])

    @pl.when(k == chips - 1)
    def _():
        gm_ref[...] = acc[...].astype(BF16)


def mid_stage(place, own, got, go, hidden, gain, w_own, w_other, n):
    rows, width = go.shape
    chips, _, heads_cols, _ = w_own.shape
    whole = pl.BlockSpec((rows, width), lambda k, place: (0, 0))
    line = pl.BlockSpec((1, width), lambda k, place: (0, 0))
    block = pl.BlockSpec((1,) + w_own.shape[1:], lambda k, place: (k, 0, 0, 0))
    return call(
        functools.partial(mid_kernel, n, chips),
        pltpu.PrefetchScalarGridSpec(
            num_scalar_prefetch=1,
            grid=(chips,),
            in_specs=[whole, whole, whole, line, block, block] + [whole] * len(got),
            out_specs=[
                pl.BlockSpec((n, rows, heads_cols), lambda k, place: (0, 0, 0)),
                whole,
                whole,
                line,
            ],
            scratch_shapes=[pltpu.VMEM((n, rows, heads_cols), F32)],
        ),
        [
            shape((n, rows, heads_cols), BF16),
            shape((rows, width), F32),
            shape((rows, width), BF16),
            shape((1, width), F32),
        ],
        4 * rows * w_own.size,
        4 * w_own.size + 20 * rows * width,
    )(place, own, go, hidden, gain, w_own, w_other, *got)


def out_weight_kernel(n, count, place_ref, *refs):
    mixed_refs, mid_ref, out_refs = refs[:n], refs[n], refs[len(refs) - count * count :]
    cols = mid_ref.shape[1] // count
    for s in range(n):
        grad = mm_tn(mixed_refs[s][...], mid_ref[...])
        t = lax.rem(place_ref[0] - s + n, n)
        if count == 1:
            out_refs[0][0, t] = grad.astype(BF16)
            continue
        grad = (grad + refs[n + 1][0, t].astype(F32)).astype(BF16)
        for piece in range(count):
            rows = n // count

            @pl.when((t >= piece * rows) & (t < (piece + 1) * rows))
            def _(piece=piece, rows=rows, grad=grad, t=t):
                for half in range(count):
                    out_refs[count * piece + half][0, t - piece * rows] = grad[
                        :, half * cols : (half + 1) * cols
                    ]


def out_weight_grad(place, side, mixed, mid, n, chips, got):
    rows, width = mid.shape
    cols = mixed[0].shape[1]
    own = width // (2 * chips)
    count = 1 if got is None else 2
    block = lambda count: pl.BlockSpec(
        (1, n // count, cols, own // count), lambda c, place: (c, 0, 0, 0)
    )
    extra = [] if got is None else [got]
    return call(
        functools.partial(out_weight_kernel, n, count),
        pltpu.PrefetchScalarGridSpec(
            num_scalar_prefetch=1,
            grid=(chips,),
            in_specs=[pl.BlockSpec((rows, cols), lambda c, place: (0, 0))] * n
            + [pl.BlockSpec((rows, own), lambda c, place: (0, 2 * c + place[3]))]
            + [block(1)] * len(extra),
            out_specs=[block(count)] * count**2,
        ),
        [shape((chips, n // count, cols, own // count), BF16)] * count**2,
        rows * width * cols * n,
        n * cols * width,
    )(jnp.concatenate([place, side]), *mixed, mid, *extra)


def entry_kernel(sid_ref, grad_ref, w_ref, out_ref):
    out_ref[...] = mm_nt(grad_ref[...], w_ref[...]).astype(BF16)


def entry_shard(sid, grads, w_qkv, rows):
    width, cols = w_qkv.shape
    tile = width // 4
    return call(
        entry_kernel,
        pltpu.PrefetchScalarGridSpec(
            num_scalar_prefetch=1,
            grid=(4,),
            in_specs=[
                pl.BlockSpec((rows, cols), lambda j, sid: (sid[0], 0)),
                pl.BlockSpec((tile, cols), lambda j, sid: (j, 0)),
            ],
            out_specs=pl.BlockSpec((rows, tile), lambda j, sid: (0, j)),
        ),
        shape((rows, width), BF16),
        2 * rows * width * cols,
        2 * (width * cols + rows * cols + rows * width),
    )(sid, grads, w_qkv)


def rows_grad_kernel(count, x_ref, *refs):
    out_ref = refs[-1]
    units = refs[0].shape[1]
    for j, ref in enumerate(refs[:count]):
        out_ref[0, :, j * units : (j + 1) * units] = mm_tn(x_ref[...], ref[...]).astype(BF16)


def rows_grad(x, factors, place, batches, kept):
    block_rows, width = x.shape
    units = factors[0].shape[1]
    rows = width // batches
    count = len(factors)
    extra = [] if kept is None else [kept]
    return call(
        functools.partial(rows_grad_kernel, count),
        pltpu.PrefetchScalarGridSpec(
            num_scalar_prefetch=0,
            grid=(batches,),
            in_specs=[pl.BlockSpec((block_rows, rows), lambda j: (0, j))]
            + [pl.BlockSpec((block_rows, units), lambda j: (0, 0))] * count
            + [pl.BlockSpec(memory_space=pl.ANY)] * len(extra),
            out_specs=pl.BlockSpec((1, rows, count * units), lambda j: (j, 0, place)),
        ),
        shape((batches, rows, 3 * units), BF16),
        2 * block_rows * width * units * count,
        2 * (block_rows * width + count * (block_rows + width) * units),
        {1 + count: 0} if extra else None,
    )(x, *factors, *extra)


def qkv_weight_kernel(side_ref, entry_ref, grad_ref, w_ref, out_ref, part_ref):
    grad = mm_tn(entry_ref[...], grad_ref[...])
    out_ref[0] = grad.astype(BF16)
    both = grad * w_ref[...].astype(F32)
    lanes = part_ref.shape[2]
    total = both[:, :lanes]
    for first in range(lanes, both.shape[1], lanes):
        total = total + both[:, first : first + lanes]
    part_ref[0] = total


def qkv_weight_grad(side, entry, grads, w_qkv, chips):
    block_rows, width = entry.shape
    cols = grads.shape[1]
    rows = width // (2 * chips)
    return call(
        qkv_weight_kernel,
        pltpu.PrefetchScalarGridSpec(
            num_scalar_prefetch=1,
            grid=(chips,),
            in_specs=[
                pl.BlockSpec((block_rows, rows), lambda j, side: (0, 2 * j + side[0])),
                pl.BlockSpec((block_rows, cols), lambda j, side: (0, 0)),
                pl.BlockSpec((rows, cols), lambda j, side: (2 * j + side[0], 0)),
            ],
            out_specs=[
                pl.BlockSpec((1, rows, cols), lambda j, side: (j, 0, 0)),
                pl.BlockSpec((1, rows, 128), lambda j, side: (j, 0, 0)),
            ],
        ),
        [shape((chips, rows, cols), BF16), shape((chips, rows, 128), F32)],
        block_rows * width * cols,
        2 * (block_rows * width + block_rows * cols + 2 * width * cols),
    )(side, entry, grads, w_qkv)


def exchange(value, axis, step):
    size = lax.axis_size(axis)
    return lax.ppermute(value, axis, [(i, i ^ step) for i in range(size)])


def total_over(value, axis):
    step = 1
    while step < lax.axis_size(axis):
        value = value + exchange(value, axis, step)
        step *= 2
    return value


@jax.tree_util.register_pytree_node_class
class Halves:
    def __init__(self, values, axes):
        self.values, self.axes = tuple(values), tuple(axes)

    def tree_flatten(self):
        return self.values, self.axes

    @classmethod
    def tree_unflatten(cls, axes, values):
        return cls(values, axes)

    def orders(self, batches):
        bits = tuple(range(1, batches.bit_length() - 1))
        return bits, bits[::-1]

    def send(self, step, batches):
        done = [send_half(v, a, o[step]) for v, a, o in zip(self.values, self.axes, self.orders(batches))]
        kept, got, axes = zip(*done)
        return Halves(kept, axes), got

    def add(self, got):
        values = [v.astype(F32) + g.astype(F32) for v, g in zip(self.values, got)]
        return Halves(values, self.axes)

    def double(self, step, batches):
        done = []
        for value, axes, order in zip(self.values, self.axes, self.orders(batches)):
            got = exchange(value, DP, 1 << order[step])
            done.append((jnp.stack([value, got]), (order[step],) + axes))
        return Halves(*zip(*done))

    def pieces(self, batches):
        bits = self.orders(batches)[1]
        done = []
        for value, axes in zip(self.values, self.axes):
            rest = list(range(len(axes), value.ndim))
            value = value.transpose([axes.index(bit) for bit in bits] + rest)
            done.append(value.reshape((batches // 2,) + value.shape[len(axes) :]))
        return jnp.concatenate(done, axis=2)


def send_half(value, axes, bit):
    own = lax.rem(lax.div(lax.axis_index(DP), 1 << bit), 2)
    at = axes.index(bit)
    sent = lax.dynamic_index_in_dim(value, 1 - own, at, False).astype(BF16)
    kept = lax.dynamic_index_in_dim(value, own, at, False)
    return kept, exchange(sent, DP, 1 << bit), axes[:at] + axes[at + 1 :]


def halves_of(first, second):
    bits = first.shape[0].bit_length() - 1
    axes = tuple(range(1, bits + 1))[::-1]
    return Halves([v.reshape((2,) * bits + v.shape[1:]) for v in (first, second)], (axes, axes))


def join(*values):
    return lax.optimization_barrier(values)


def add_low(a, b):
    return (a.astype(F32) + b.astype(F32)).astype(BF16)


class RingSum:
    def __init__(self, shift):
        self.parts, self.shift, self.step, self.moving = [], shift, 0, None

    def add(self):
        self.step += 1
        if self.step < len(self.parts):
            part = self.parts[self.step]
            self.moving = part if self.step == 1 else add_low(self.moving, part)

    def send(self):
        if self.step < len(self.parts):
            self.moving = self.shift(self.moving)

    def hop(self):
        self.add()
        self.send()


def total_of(own, got):
    total = own.astype(F32)
    for value in got:
        total = total + value.astype(F32)
    return total


def local(
    tokens,
    seq_lengths,
    attn_gain,
    mlp_gain,
    q_gain,
    k_gain,
    w_query,
    key_weight,
    value_weight,
    w_out,
    w_gate,
    w_up,
    w_down,
    out_grad,
):
    n = lax.axis_size("tensor")
    batches = lax.axis_size(DP)
    rows, width = tokens.shape
    block_rows = rows * n
    dim = q_gain.shape[0]
    heads = w_query.shape[1] // dim
    kv_heads = key_weight.shape[1] // dim
    z = lax.axis_index("tensor").astype(jnp.int32)
    zs = z.reshape(1)
    ring = [(i, (i + 1) % n) for i in range(n)]
    shift = lambda v, d=1: lax.ppermute(v, "tensor", [(i, (i + d) % n) for i in range(n)])
    shard_of = lambda s: lax.rem(z - s + n, n).reshape(1)

    chips = batches // 2
    core = lax.axis_index("core").astype(jnp.int32).reshape(1)
    place = jnp.stack([z, lax.axis_index("chip").astype(jnp.int32), core[0]])
    steps = batches.bit_length() - 2

    own_cols = width // batches
    piece = lax.dynamic_slice_in_dim(w_out, lax.axis_index(DP) * own_cols, own_cols, 1)
    piece = lax.all_gather(piece, "tensor", axis=0, tiled=False)

    offset, position = positions_of(seq_lengths[0], block_rows)
    start = offset[None, :]
    cosine, sine = rope_tables(position, dim)
    w_qkv = jnp.concatenate([w_query, key_weight, value_weight], axis=1)
    gain_one, gain_two = attn_gain[None, :], mlp_gain[None, :]
    qg, kg = q_gain[None, :], k_gain[None, :]

    came = shift(tokens)
    came, piece, w_qkv, cosine, sine, start = join(came, piece, w_qkv, cosine, sine, start)
    blocks = [tokens, came]
    middle = piece.shape[1] // 2
    halves = Halves((piece[:, :middle], piece[:, middle:]), ((), ()))
    kept, ready = None, 0
    for s in range(1, n):
        came = shift(blocks[s]) if s < n - 1 else None
        while ready <= s:
            kept = qkv_shard(
                shard_of(ready), blocks[ready], gain_one, w_qkv, cosine, sine, qg, kg, heads, kv_heads,
                dim, block_rows, kept,
            )
            ready += 1
        if s <= steps:
            halves = halves.double(s - 1, batches)
        if came is not None:
            came, kept, halves = join(came, kept, halves)
            blocks.append(came)
    entry_all, side, raw = kept
    w_own = halves.pieces(batches)
    w_other = exchange(w_own, "core", 1)

    later_grad, _ = join(out_grad, blocks[-1])
    grad_all = lax.all_gather(later_grad, "tensor", axis=0, tiled=True)

    mixed, lse = attention_forward(zs, side, start, n, heads, kv_heads, dim)
    mixed, w_own = join(mixed, w_own)
    mixed = [mixed[0]] + [shift(mixed[d], d) for d in range(1, n)]
    mixed, w_other = join(mixed, w_other)
    hidden, mlp_entry = out_projection(place, mixed, w_own, w_other, tokens, gain_two, n)

    weights = (w_gate, w_up, w_down)
    inner_sum = RingSum(shift)
    down_one, down_two, down_parts = RingSum(shift), RingSum(shift), []
    over_dp = lambda g: lax.psum_scatter(g, DP, scatter_dimension=0, tiled=False)
    blocks, kept = [mlp_entry], None
    for t in range(2 * n - 2):
        if t < n - 1:
            blocks.append(shift(blocks[t]))
        if t >= n - 1:
            inner_sum.hop()
        s = (0, -1)[t] if t < 2 else t - 1
        if 0 <= s < n:
            kept, down, inner = mlp_shard(
                shard_of(s), blocks[s], grad_all if s else out_grad, weights, kept, block_rows
            )
            down_parts.append(down)
            inner_sum.parts.append(inner)
        if s >= n:
            down_one.parts = [part[:, : width // 2] for part in down_parts]
            down_two.parts = [part[:, width // 2 :] for part in down_parts]
            down_one.hop()
            mlp_grads = rows_grad(grad_all, [active], 2, batches, None)
            mlp_grads = rows_grad(mlp_all, [gate_grad, up_grad], 0, batches, mlp_grads)
            inner_sum.moving, down_one.moving, mlp_grads = join(
                inner_sum.moving, down_one.moving, mlp_grads
            )
            mlp_grads = over_dp(mlp_grads)
        else:
            state = (blocks, kept, inner_sum.parts, inner_sum.moving)
            state, grad_all = join(state, grad_all) if t else (join(*state), grad_all)
            blocks, kept, inner_sum.parts, inner_sum.moving = state
            active, gate_grad, up_grad, mlp_all = kept

    down_two.hop()
    gm, grad_hidden, grad_mid, mlp_part = mid_stage(
        place, inner_sum.parts[0], (inner_sum.moving,), out_grad, hidden, gain_two, w_own, w_other, n
    )
    gm, grad_mid, down_two.moving = join(gm, grad_mid, down_two.moving)

    gm = [gm[0]] + [shift(gm[d], d) for d in range(1, n)]
    (got,) = out_weight_grad(place, 1 - core, mixed, grad_mid, n, chips, None)
    down_one.add()
    down_two.add()
    gm, got, down_one.moving, down_two.moving = join(gm, got, down_one.moving, down_two.moving)

    down_one.send()
    got = exchange(got, "core", 1)
    grads, gain_parts = attention_backward(
        zs, gm, side, raw, lse, start, cosine, sine, qg, kg, heads, kv_heads, dim
    )
    grads, got, down_one.moving = join(grads, got, down_one.moving)
    down_two.send()
    down_one.hop()
    entry_part = lambda s: entry_shard(shard_of(s), grads, w_qkv, rows)
    entry_sum = RingSum(shift)
    entry_sum.parts = [None, entry_part(1)] + [None] * (n - 2)
    w_out_grad = out_weight_grad(place, core, mixed, grad_mid, n, chips, got)
    entry_sum.parts[1], grads, w_out_grad, down_one.moving, down_two.moving = join(
        entry_sum.parts[1], grads, w_out_grad, down_one.moving, down_two.moving
    )

    out_one, out_two = halves_of(*w_out_grad[:2]), halves_of(*w_out_grad[2:])
    entry_sum.add()

    entry_sum.send()
    down_two.hop()
    out_one, one_got = out_one.send(0, batches)
    qkv_sent, lanes_sent = qkv_weight_grad(1 - core, entry_all, grads, w_qkv, chips)
    w_qkv_grad, lanes = qkv_weight_grad(core, entry_all, grads, w_qkv, chips)
    entry_sum.parts[2 % n] = entry_part(2 % n)
    entry_sum.add()
    state = (entry_sum.moving, down_two.moving, qkv_sent, w_qkv_grad)
    state, grads, lanes, lanes_sent, out_one, one_got, out_two = join(
        state, grads, lanes, lanes_sent, out_one, one_got, out_two
    )
    entry_sum.moving, down_two.moving, qkv_sent, w_qkv_grad = state
    lanes, lanes_sent = jnp.sum(lanes, axis=2), jnp.sum(lanes_sent, axis=2)
    lanes = jnp.where(core[0] == 0, jnp.stack([lanes, lanes_sent], 1), jnp.stack([lanes_sent, lanes], 1))
    attn_part = lanes.reshape(width) / attn_gain
    totals = jnp.concatenate([attn_part, mlp_part[0], gain_parts[0], gain_parts[1]])[None, :]

    entry_sum.send()
    out_two, two_got = out_two.send(0, batches)
    qkv_got = exchange(qkv_sent, "core", 1)
    totals = total_over(totals, DP)
    entry_sum.parts[3 % n] = entry_part(3 % n)
    entry_sum.add()
    while down_one.step < n - 1:
        down_one.hop()
        down_two.hop()
    moved = jnp.concatenate([down_one.moving, down_two.moving], axis=1)
    output = total_of(hidden, [down_parts[0], moved]).astype(BF16)
    state = (entry_sum.moving, out_one, one_got, out_two, two_got, qkv_got, w_qkv_grad)
    state, grads, totals, output = join(state, grads, totals, output)
    entry_sum.moving, out_one, one_got, out_two, two_got, qkv_got, w_qkv_grad = state

    out_one, out_two = out_one.add(one_got), out_two.add(two_got)
    values = [jnp.concatenate(pair, axis=-3) for pair in zip(out_one.values, out_two.values)]
    out_halves = Halves(values, out_one.axes)
    for step in range(1, steps):
        out_halves, out_got = out_halves.send(step, batches)
        out_got, w_qkv_grad, qkv_got = join(out_got, w_qkv_grad, qkv_got)
        out_halves = out_halves.add(out_got)
    w_out_grad = jnp.concatenate(out_halves.values, axis=-1).astype(BF16)
    out_sum = RingSum(shift)
    out_sum.parts = [lax.dynamic_index_in_dim(w_out_grad, shard_of(d)[0], 0, False) for d in range(n)]
    for _ in range(n - 1):
        out_sum.hop()
    middle = w_qkv_grad.shape[-1] // 2
    qkv_halves = halves_of(
        add_low(w_qkv_grad[..., :middle], qkv_got[..., :middle]),
        add_low(w_qkv_grad[..., middle:], qkv_got[..., middle:]),
    )
    for step in range(steps):
        qkv_halves, qkv_got = qkv_halves.send(step, batches)
        if step < steps - 1:
            qkv_halves = qkv_halves.add(qkv_got)
    totals = total_over(totals, "tensor")
    for s in range(3, n):
        entry_sum.send()
        entry_sum.parts[(s + 1) % n] = entry_part((s + 1) % n)
        if s < n - 1:
            entry_sum.add()
            entry_sum.moving, grads = join(entry_sum.moving, grads)
    grad_entry = total_of(entry_sum.parts[0], [entry_sum.moving])
    units = w_gate.shape[1]
    mlp_grads = mlp_grads.astype(F32)
    mlp_grads = mlp_grads[:, :units], mlp_grads[:, units : 2 * units], mlp_grads[:, 2 * units :].T
    out_sum.moving, mlp_grads = join(out_sum.moving, mlp_grads)
    w_out_grad = total_of(out_sum.parts[0], [out_sum.moving])
    w_qkv_grad = jnp.concatenate(qkv_halves.add(qkv_got).values, axis=-1)

    x = tokens.astype(F32)
    scale = inv_root_of(x)
    token_grad = (grad_hidden + norm_back(grad_entry * attn_gain, x * scale, scale)).astype(BF16)

    totals = totals[0]
    attn_gain_grad = totals[:width]
    mlp_gain_grad = totals[width : 2 * width]
    q_gain_grad = totals[2 * width : 2 * width + dim]
    k_gain_grad = totals[2 * width + dim :]
    a, b = heads * dim, (heads + kv_heads) * dim
    return (
        output,
        token_grad,
        attn_gain_grad,
        mlp_gain_grad,
        q_gain_grad,
        k_gain_grad,
        w_qkv_grad[:, :a],
        w_qkv_grad[:, a:b],
        w_qkv_grad[:, b:],
        w_out_grad,
        *mlp_grads,
    )


def solution(mesh):
    batches, shards = mesh.shape["dp"], mesh.shape["tensor"]
    return jax.shard_map(
        local,
        mesh=Mesh(mesh.devices.reshape(batches // 2, 2, shards), DP + ("tensor",)),
        in_specs=(
            P(("chip", "core", "tensor"), None),
            P(DP, None),
            P(),
            P(),
            P(),
            P(),
            P(None, "tensor"),
            P(None, "tensor"),
            P(None, "tensor"),
            P("tensor", None),
            P(None, "tensor"),
            P(None, "tensor"),
            P("tensor", None),
            P(("chip", "core", "tensor"), None),
        ),
        out_specs=(
            P(("chip", "core", "tensor"), None),
            P(("chip", "core", "tensor"), None),
            P(),
            P(),
            P(),
            P(),
            P(DP, "tensor"),
            P(DP, "tensor"),
            P(DP, "tensor"),
            P("tensor", DP),
            P(DP, "tensor"),
            P(DP, "tensor"),
            P("tensor", DP),
        ),
        check_vma=False,
    )
```

```python
import functools

import jax
import jax.numpy as jnp
from jax import lax
from jax.experimental import pallas as pl
from jax.experimental.pallas import tpu as pltpu
from jax.sharding import Mesh, PartitionSpec as P

NORM_EPSILON = 1e-06
ROPE_BASE = 1000000.0
MASK_FILL = -1e30
VMEM_BYTES = 52 * 1024 * 1024
F32 = jnp.float32
BF16 = jnp.bfloat16
DP = ("chip", "core")
COST = 1000

NT = (((1,), (1,)), ((), ()))
TN = (((0,), (0,)), ((), ()))


def mm(a, b):
    return jnp.dot(a, b, preferred_element_type=F32)


def mm_nt(a, b):
    return lax.dot_general(a, b, NT, preferred_element_type=F32)


def mm_tn(a, b):
    return lax.dot_general(a, b, TN, preferred_element_type=F32)


def inv_root_of(values):
    return lax.rsqrt(jnp.mean(values * values, axis=-1, keepdims=True) + NORM_EPSILON)


def norm_back(grad_normed, normal, inv_root):
    return inv_root * (
        grad_normed - normal * jnp.mean(grad_normed * normal, axis=-1, keepdims=True)
    )


def call(kernel, grid_spec, out_shape, flops, nbytes, aliases=None):
    return pl.pallas_call(
        kernel,
        grid_spec=grid_spec,
        out_shape=out_shape,
        input_output_aliases=aliases or {},
        compiler_params=pltpu.CompilerParams(vmem_limit_bytes=VMEM_BYTES),
        cost_estimate=pl.CostEstimate(flops=flops // COST, bytes_accessed=nbytes // COST, transcendentals=0),
    )


def shape(dims, dtype):
    return jax.ShapeDtypeStruct(dims, dtype)


def positions_of(lengths, count_of_rows):
    seq_ends = jnp.cumsum(lengths, dtype=jnp.int32)
    starts = seq_ends - lengths
    place_index = jnp.arange(count_of_rows, dtype=jnp.int32)
    segment = jnp.sum(
        (place_index[:, None] >= seq_ends[None, :]).astype(jnp.int32), axis=1, dtype=jnp.int32
    )
    belongs = segment[:, None] == jnp.arange(lengths.shape[0], dtype=jnp.int32)[None, :]
    offset = jnp.sum(jnp.where(belongs, starts[None, :], 0), axis=1, dtype=jnp.int32)
    return (offset, place_index - offset)


def rope_tables(position, head_width):
    half_width = head_width // 2
    frequency = ROPE_BASE ** (-2.0 * jnp.arange(half_width, dtype=F32) / head_width)
    angles = position.astype(F32)[:, None] * frequency[None, :]
    cosine, sine = jnp.cos(angles), jnp.sin(angles)
    return (
        jnp.concatenate([cosine, cosine], axis=1),
        jnp.concatenate([-sine, sine], axis=1),
    )


def qkv_kernel(heads, kv_heads, dim, sid_ref, x_ref, gain_ref, w_ref, cos_ref, sin_ref, qg_ref, kg_ref, *refs):
    entry_ref, side_ref, raw_ref = refs[-3:]
    x = x_ref[...].astype(F32)
    entry = (x * inv_root_of(x) * gain_ref[...]).astype(BF16)
    entry_ref[...] = entry
    both = mm(entry, w_ref[...])
    cosine, sine = cos_ref[...], sin_ref[...]
    for h in range(heads + kv_heads):
        cols = slice(h * dim, (h + 1) * dim)
        raw = both[:, cols]
        raw_ref[:, cols] = raw.astype(BF16)
        gain = qg_ref[...] if h < heads else kg_ref[...]
        u = raw * inv_root_of(raw) * gain
        turned = u * cosine + pltpu.roll(u, dim // 2, 1) * sine
        if h < heads:
            turned = turned * dim ** (-0.5)
        side_ref[:, cols] = turned.astype(BF16)
    rest = slice((heads + kv_heads) * dim, (heads + 2 * kv_heads) * dim)
    side_ref[:, rest] = both[:, rest].astype(BF16)


def qkv_shard(sid, x, gain, w_qkv, cosine, sine, q_gain, k_gain, heads, kv_heads, dim, block_rows, kept):
    rows, width = x.shape
    cols = w_qkv.shape[1]
    raw_cols = (heads + kv_heads) * dim
    whole = lambda i, sid: (0, 0)
    mine = lambda i, sid: (sid[0], 0)
    in_specs = [
        pl.BlockSpec((rows, width), whole),
        pl.BlockSpec((1, width), whole),
        pl.BlockSpec((width, cols), whole),
        pl.BlockSpec((rows, dim), mine),
        pl.BlockSpec((rows, dim), mine),
        pl.BlockSpec((1, dim), whole),
        pl.BlockSpec((1, dim), whole),
    ]
    args = [sid, x, gain, w_qkv, cosine, sine, q_gain, k_gain]
    aliases = {}
    if kept is not None:
        for j, array in enumerate(kept):
            aliases[len(args)] = j
            args.append(array)
            in_specs.append(pl.BlockSpec(memory_space=pl.ANY))
    return call(
        functools.partial(qkv_kernel, heads, kv_heads, dim),
        pltpu.PrefetchScalarGridSpec(
            num_scalar_prefetch=1,
            grid=(1,),
            in_specs=in_specs,
            out_specs=[
                pl.BlockSpec((rows, width), mine),
                pl.BlockSpec((rows, cols), mine),
                pl.BlockSpec((rows, raw_cols), mine),
            ],
        ),
        [
            shape((block_rows, width), BF16),
            shape((block_rows, cols), BF16),
            shape((block_rows, raw_cols), BF16),
        ],
        2 * rows * width * cols,
        2 * (2 * rows * width + width * cols + 2 * rows * cols),
        aliases,
    )(*args)


def visible_keys(start_ref, first_row, rows, keys):
    key = lax.broadcasted_iota(jnp.int32, (keys, rows), 0)
    query = first_row + lax.broadcasted_iota(jnp.int32, (keys, rows), 1)
    return (key <= query) & (key >= start_ref[:, first_row : first_row + rows])


def attention_kernel(n, heads, kv_heads, dim, z_ref, side_ref, start_ref, mixed_ref, lse_ref):
    rows = side_ref.shape[0] // n
    group = heads // kv_heads
    for i in range(n):
        slot = lax.rem(i - z_ref[0] + n, n)
        keys = (i + 1) * rows
        here = slice(i * rows, (i + 1) * rows)
        visible = visible_keys(start_ref, i * rows, rows, keys)
        for h in range(heads):
            kv = h // group
            key = side_ref[:keys, (heads + kv) * dim : (heads + kv + 1) * dim]
            value = side_ref[
                :keys, (heads + kv_heads + kv) * dim : (heads + kv_heads + kv + 1) * dim
            ]
            cols = slice(h * dim, (h + 1) * dim)
            scores = jnp.where(visible, mm_nt(key, side_ref[here, cols]), MASK_FILL)
            peak = jnp.max(scores, axis=0, keepdims=True)
            spread = jnp.exp(scores - peak)
            total = jnp.sum(spread, axis=0, keepdims=True)
            mixed = mm_tn(value, spread.astype(BF16)) / total
            mixed_ref[slot, :, cols] = mixed.T.astype(BF16)
            lse_ref[h : h + 1, here] = peak + jnp.log(total)


def attention_forward(z, side, start, n, heads, kv_heads, dim):
    block_rows = side.shape[0]
    rows = block_rows // n
    whole2 = lambda i, z: (0, 0)
    return call(
        functools.partial(attention_kernel, n, heads, kv_heads, dim),
        pltpu.PrefetchScalarGridSpec(
            num_scalar_prefetch=1,
            grid=(1,),
            in_specs=[
                pl.BlockSpec(side.shape, whole2),
                pl.BlockSpec((1, block_rows), whole2),
            ],
            out_specs=[
                pl.BlockSpec((n, rows, heads * dim), lambda i, z: (0, 0, 0)),
                pl.BlockSpec((heads, block_rows), whole2),
            ],
        ),
        [shape((n, rows, heads * dim), BF16), shape((heads, block_rows), F32)],
        2 * block_rows * block_rows * heads * dim * 2,
        2 * side.size + 6 * block_rows * heads * dim,
    )(z, side, start)


def attention_back_kernel(n, heads, kv_heads, dim, z_ref, *refs):
    gm_refs = refs[:n]
    side_ref, raw_ref, lse_ref, start_ref, cos_ref, sin_ref, qg_ref, kg_ref = refs[n : n + 8]
    out_ref, gain_ref, gm_ref, key_acc, value_acc = refs[n + 8 :]
    block_rows = side_ref.shape[0]
    rows = block_rows // n
    group = heads // kv_heads
    q_sum = jnp.zeros((1, dim), F32)
    k_sum = jnp.zeros((1, dim), F32)
    for slot, ref in enumerate(gm_refs):
        gm_ref[slot] = ref[...]
    for kv in range(kv_heads):
        key_cols = slice((heads + kv) * dim, (heads + kv + 1) * dim)
        value_cols = slice((heads + kv_heads + kv) * dim, (heads + kv_heads + kv + 1) * dim)
        key_acc[...] = jnp.zeros_like(key_acc)
        value_acc[...] = jnp.zeros_like(value_acc)
        for i in range(n):
            slot = lax.rem(z_ref[0] - i + n, n)
            keys = (i + 1) * rows
            here = slice(i * rows, (i + 1) * rows)
            key = side_ref[:keys, key_cols]
            value = side_ref[:keys, value_cols]
            visible = visible_keys(start_ref, i * rows, rows, keys)
            cosine, sine = cos_ref[here, :], sin_ref[here, :]
            for g in range(group):
                h = kv * group + g
                cols = slice(h * dim, (h + 1) * dim)
                query = side_ref[here, cols]
                grad = gm_ref[slot, :, cols]
                scores = jnp.where(visible, mm_nt(key, query), MASK_FILL)
                soft = jnp.exp(scores - lse_ref[h : h + 1, here])
                grad_weights = mm_nt(value, grad)
                inner = jnp.sum(soft * grad_weights, axis=0, keepdims=True)
                grad_scores = (soft * (grad_weights - inner)).astype(BF16)
                value_acc[:keys, :] += mm(soft.astype(BF16), grad)
                key_acc[:keys, :] += mm(grad_scores, query)
                turned = mm_tn(key, grad_scores).T * dim ** (-0.5)
                back = turned * cosine - pltpu.roll(turned, dim // 2, 1) * sine
                raw = raw_ref[here, cols].astype(F32)
                scale = inv_root_of(raw)
                normal = raw * scale
                q_sum = q_sum + jnp.sum(back * normal, axis=0, keepdims=True)
                out_ref[here, cols] = norm_back(back * qg_ref[...], normal, scale).astype(BF16)
        turned = key_acc[...]
        back = turned * cos_ref[...] - pltpu.roll(turned, dim // 2, 1) * sin_ref[...]
        raw = raw_ref[:, key_cols].astype(F32)
        scale = inv_root_of(raw)
        normal = raw * scale
        k_sum = k_sum + jnp.sum(back * normal, axis=0, keepdims=True)
        out_ref[:, key_cols] = norm_back(back * kg_ref[...], normal, scale).astype(BF16)
        out_ref[:, value_cols] = value_acc[...].astype(BF16)
    gain_ref[...] = jnp.concatenate([q_sum, k_sum, jnp.zeros((6, dim), F32)], axis=0)


def attention_backward(z, gm, side, raw, lse, start, cosine, sine, q_gain, k_gain, heads, kv_heads, dim):
    n = len(gm)
    block_rows = side.shape[0]
    whole2 = lambda i, z: (0, 0)
    ins = (*gm, side, raw, lse, start, cosine, sine, q_gain, k_gain)
    return call(
        functools.partial(attention_back_kernel, n, heads, kv_heads, dim),
        pltpu.PrefetchScalarGridSpec(
            num_scalar_prefetch=1,
            grid=(1,),
            in_specs=[pl.BlockSpec(a.shape, whole2) for a in ins],
            out_specs=[pl.BlockSpec(side.shape, whole2), pl.BlockSpec((8, dim), whole2)],
            scratch_shapes=[
                pltpu.VMEM((n,) + gm[0].shape, BF16),
                pltpu.VMEM((block_rows, dim), F32),
                pltpu.VMEM((block_rows, dim), F32),
            ],
        ),
        [shape(side.shape, BF16), shape((8, dim), F32)],
        2 * block_rows * block_rows * heads * dim * 5,
        12 * side.size,
    )(z, *ins)


def column_block(place_ref, k, other, cols):
    block = 2 * lax.bitwise_xor(place_ref[1], k) + (1 - place_ref[2] if other else place_ref[2])
    return pl.ds(pl.multiple_of(block * cols, cols), cols)


def out_kernel(n, chips, place_ref, *refs):
    mixed_refs = refs[:n]
    own_ref, other_ref, x_ref, gain_ref, hidden_ref, entry_ref, acc = refs[n:]
    k = pl.program_id(0)
    for other, w_ref in enumerate((own_ref, other_ref)):
        part = mm(mixed_refs[0][...], w_ref[0, place_ref[0]])
        for s in range(1, n):
            part = part + mm(mixed_refs[s][...], w_ref[0, lax.rem(place_ref[0] - s + n, n)])
        acc[:, column_block(place_ref, k, other, part.shape[1])] = part

    @pl.when(k == chips - 1)
    def _():
        hidden = acc[...] + x_ref[...].astype(F32)
        hidden_ref[...] = hidden
        entry_ref[...] = (hidden * inv_root_of(hidden) * gain_ref[...]).astype(BF16)


def out_projection(place, mixed, w_own, w_other, x, gain, n):
    rows, width = x.shape
    chips = w_own.shape[0]
    whole = lambda k, place: (0, 0)
    block = pl.BlockSpec((1,) + w_own.shape[1:], lambda k, place: (k, 0, 0, 0))
    return call(
        functools.partial(out_kernel, n, chips),
        pltpu.PrefetchScalarGridSpec(
            num_scalar_prefetch=1,
            grid=(chips,),
            in_specs=[pl.BlockSpec(mixed[0].shape, whole)] * n
            + [
                block,
                block,
                pl.BlockSpec((rows, width), whole),
                pl.BlockSpec((1, width), whole),
            ],
            out_specs=[pl.BlockSpec((rows, width), whole), pl.BlockSpec((rows, width), whole)],
            scratch_shapes=[pltpu.VMEM((rows, width), F32)],
        ),
        [shape((rows, width), F32), shape((rows, width), BF16)],
        4 * rows * w_own.size,
        4 * w_own.size + 10 * rows * width,
    )(place, *mixed, w_own, w_other, x, gain)


def mlp_kernel(tiles, sid_ref, x_ref, go_ref, wg_ref, wu_ref, wd_ref, *refs):
    active_ref, gate_grad_ref, up_grad_ref, copy_ref, down_ref, inner_ref, down_acc, inner_acc = refs[-8:]
    j = pl.program_id(0)
    x = x_ref[...]
    gate = mm(x, wg_ref[...])
    up = mm(x, wu_ref[...])
    sigmoid = jax.nn.sigmoid(gate)
    silu = gate * sigmoid
    active = (silu * up).astype(BF16)
    active_ref[...] = active
    grad_active = mm_nt(go_ref[...], wd_ref[...])
    gate_grad = (grad_active * up * sigmoid * (1.0 + gate * (1.0 - sigmoid))).astype(BF16)
    up_grad = (grad_active * silu).astype(BF16)
    gate_grad_ref[...] = gate_grad
    up_grad_ref[...] = up_grad
    inner = mm_nt(gate_grad, wg_ref[...]) + mm_nt(up_grad, wu_ref[...])
    down = mm(active, wd_ref[...])

    @pl.when(j == 0)
    def _():
        copy_ref[...] = x
        inner_acc[...] = inner
        down_acc[...] = down

    @pl.when(j > 0)
    def _():
        inner_acc[...] += inner
        down_acc[...] += down

    @pl.when(j == tiles - 1)
    def _():
        inner_ref[...] = inner_acc[...].astype(BF16)
        down_ref[...] = down_acc[...].astype(BF16)


def mlp_shard(sid, x, grads, weights, kept, block_rows):
    w_gate, w_up, w_down = weights
    rows, width = x.shape
    units = w_gate.shape[1]
    tile = next(t for t in (512, 384, 256, 128) if units % t == 0)
    tiles = units // tile
    whole = pl.BlockSpec((rows, width), lambda j, sid: (0, 0))
    mine = pl.BlockSpec((rows, width), lambda j, sid: (sid[0], 0))
    tiled = pl.BlockSpec((rows, tile), lambda j, sid: (sid[0], j))
    column = pl.BlockSpec((width, tile), lambda j, sid: (0, j))
    in_specs = [
        whole,
        whole if grads.shape[0] == rows else mine,
        column,
        column,
        pl.BlockSpec((tile, width), lambda j, sid: (j, 0)),
    ]
    args = [sid.reshape(1), x, grads, w_gate, w_up, w_down]
    aliases = {}
    if kept is not None:
        for j, array in enumerate(kept):
            aliases[len(args)] = j
            args.append(array)
            in_specs.append(pl.BlockSpec(memory_space=pl.ANY))
    *kept, down, inner = call(
        functools.partial(mlp_kernel, tiles),
        pltpu.PrefetchScalarGridSpec(
            num_scalar_prefetch=1,
            grid=(tiles,),
            in_specs=in_specs,
            out_specs=[tiled] * 3 + [mine] + [whole] * 2,
            scratch_shapes=[pltpu.VMEM((rows, width), F32), pltpu.VMEM((rows, width), F32)],
        ),
        [shape((block_rows, units), BF16)] * 3
        + [shape((block_rows, width), BF16)]
        + [shape((rows, width), BF16)] * 2,
        2 * rows * width * units * 6,
        2 * (3 * width * units + 3 * rows * units + 5 * rows * width),
        aliases,
    )(*args)
    return kept, down, inner


def mid_kernel(n, chips, place_ref, own_part_ref, go_ref, hidden_ref, gain_ref, own_ref, other_ref, *refs):
    got_refs = refs[:-5]
    gm_ref, gh_ref, mid_ref, part_ref, acc = refs[-5:]
    k = pl.program_id(0)

    @pl.when(k == 0)
    def _():
        hidden = hidden_ref[...]
        scale = inv_root_of(hidden)
        normal = hidden * scale
        inner = own_part_ref[...].astype(F32)
        for ref in got_refs:
            inner = inner + ref[...].astype(F32)
        part_ref[...] = jnp.sum(inner * normal, axis=0, keepdims=True)
        grad_hidden = go_ref[...].astype(F32) + norm_back(inner * gain_ref[...], normal, scale)
        gh_ref[...] = grad_hidden
        mid_ref[...] = grad_hidden.astype(BF16)
        acc[...] = jnp.zeros_like(acc)

    cols = own_ref.shape[3]
    own = mid_ref[:, column_block(place_ref, k, False, cols)]
    other = mid_ref[:, column_block(place_ref, k, True, cols)]
    for s in range(n):
        t = lax.rem(place_ref[0] + s, n)
        acc[s] += mm_nt(own, own_ref[0, t]) + mm_nt(other, other_ref[0, t])

    @pl.when(k == chips - 1)
    def _():
        gm_ref[...] = acc[...].astype(BF16)


def mid_stage(place, own, got, go, hidden, gain, w_own, w_other, n):
    rows, width = go.shape
    chips, _, heads_cols, _ = w_own.shape
    whole = pl.BlockSpec((rows, width), lambda k, place: (0, 0))
    line = pl.BlockSpec((1, width), lambda k, place: (0, 0))
    block = pl.BlockSpec((1,) + w_own.shape[1:], lambda k, place: (k, 0, 0, 0))
    return call(
        functools.partial(mid_kernel, n, chips),
        pltpu.PrefetchScalarGridSpec(
            num_scalar_prefetch=1,
            grid=(chips,),
            in_specs=[whole, whole, whole, line, block, block] + [whole] * len(got),
            out_specs=[
                pl.BlockSpec((n, rows, heads_cols), lambda k, place: (0, 0, 0)),
                whole,
                whole,
                line,
            ],
            scratch_shapes=[pltpu.VMEM((n, rows, heads_cols), F32)],
        ),
        [
            shape((n, rows, heads_cols), BF16),
            shape((rows, width), F32),
            shape((rows, width), BF16),
            shape((1, width), F32),
        ],
        4 * rows * w_own.size,
        4 * w_own.size + 20 * rows * width,
    )(place, own, go, hidden, gain, w_own, w_other, *got)


def out_weight_kernel(n, count, place_ref, *refs):
    mixed_refs, mid_ref, out_refs = refs[:n], refs[n], refs[len(refs) - count * count :]
    cols = mid_ref.shape[1] // count
    for s in range(n):
        grad = mm_tn(mixed_refs[s][...], mid_ref[...])
        t = lax.rem(place_ref[0] - s + n, n)
        if count == 1:
            out_refs[0][0, t] = grad.astype(BF16)
            continue
        grad = (grad + refs[n + 1][0, t].astype(F32)).astype(BF16)
        for piece in range(count):
            rows = n // count

            @pl.when((t >= piece * rows) & (t < (piece + 1) * rows))
            def _(piece=piece, rows=rows, grad=grad, t=t):
                for half in range(count):
                    out_refs[count * piece + half][0, t - piece * rows] = grad[
                        :, half * cols : (half + 1) * cols
                    ]


def out_weight_grad(place, side, mixed, mid, n, chips, got):
    rows, width = mid.shape
    cols = mixed[0].shape[1]
    own = width // (2 * chips)
    count = 1 if got is None else 2
    block = lambda count: pl.BlockSpec(
        (1, n // count, cols, own // count), lambda c, place: (c, 0, 0, 0)
    )
    extra = [] if got is None else [got]
    return call(
        functools.partial(out_weight_kernel, n, count),
        pltpu.PrefetchScalarGridSpec(
            num_scalar_prefetch=1,
            grid=(chips,),
            in_specs=[pl.BlockSpec((rows, cols), lambda c, place: (0, 0))] * n
            + [pl.BlockSpec((rows, own), lambda c, place: (0, 2 * c + place[3]))]
            + [block(1)] * len(extra),
            out_specs=[block(count)] * count**2,
        ),
        [shape((chips, n // count, cols, own // count), BF16)] * count**2,
        rows * width * cols * n,
        n * cols * width,
    )(jnp.concatenate([place, side]), *mixed, mid, *extra)


def entry_kernel(sid_ref, grad_ref, w_ref, out_ref):
    out_ref[...] = mm_nt(grad_ref[...], w_ref[...]).astype(BF16)


def entry_shard(sid, grads, w_qkv, rows):
    width, cols = w_qkv.shape
    tile = width // 4
    return call(
        entry_kernel,
        pltpu.PrefetchScalarGridSpec(
            num_scalar_prefetch=1,
            grid=(4,),
            in_specs=[
                pl.BlockSpec((rows, cols), lambda j, sid: (sid[0], 0)),
                pl.BlockSpec((tile, cols), lambda j, sid: (j, 0)),
            ],
            out_specs=pl.BlockSpec((rows, tile), lambda j, sid: (0, j)),
        ),
        shape((rows, width), BF16),
        2 * rows * width * cols,
        2 * (width * cols + rows * cols + rows * width),
    )(sid, grads, w_qkv)


def rows_grad_kernel(count, x_ref, *refs):
    out_ref = refs[-1]
    units = refs[0].shape[1]
    for j, ref in enumerate(refs[:count]):
        out_ref[0, :, j * units : (j + 1) * units] = mm_tn(x_ref[...], ref[...]).astype(BF16)


def rows_grad(x, factors, place, batches, kept):
    block_rows, width = x.shape
    units = factors[0].shape[1]
    rows = width // batches
    count = len(factors)
    extra = [] if kept is None else [kept]
    return call(
        functools.partial(rows_grad_kernel, count),
        pltpu.PrefetchScalarGridSpec(
            num_scalar_prefetch=0,
            grid=(batches,),
            in_specs=[pl.BlockSpec((block_rows, rows), lambda j: (0, j))]
            + [pl.BlockSpec((block_rows, units), lambda j: (0, 0))] * count
            + [pl.BlockSpec(memory_space=pl.ANY)] * len(extra),
            out_specs=pl.BlockSpec((1, rows, count * units), lambda j: (j, 0, place)),
        ),
        shape((batches, rows, 3 * units), BF16),
        2 * block_rows * width * units * count,
        2 * (block_rows * width + count * (block_rows + width) * units),
        {1 + count: 0} if extra else None,
    )(x, *factors, *extra)


def qkv_weight_kernel(side_ref, entry_ref, grad_ref, w_ref, out_ref, part_ref):
    grad = mm_tn(entry_ref[...], grad_ref[...])
    out_ref[0] = grad.astype(BF16)
    both = grad * w_ref[...].astype(F32)
    lanes = part_ref.shape[2]
    total = both[:, :lanes]
    for first in range(lanes, both.shape[1], lanes):
        total = total + both[:, first : first + lanes]
    part_ref[0] = total


def qkv_weight_grad(side, entry, grads, w_qkv, chips):
    block_rows, width = entry.shape
    cols = grads.shape[1]
    rows = width // (2 * chips)
    return call(
        qkv_weight_kernel,
        pltpu.PrefetchScalarGridSpec(
            num_scalar_prefetch=1,
            grid=(chips,),
            in_specs=[
                pl.BlockSpec((block_rows, rows), lambda j, side: (0, 2 * j + side[0])),
                pl.BlockSpec((block_rows, cols), lambda j, side: (0, 0)),
                pl.BlockSpec((rows, cols), lambda j, side: (2 * j + side[0], 0)),
            ],
            out_specs=[
                pl.BlockSpec((1, rows, cols), lambda j, side: (j, 0, 0)),
                pl.BlockSpec((1, rows, 128), lambda j, side: (j, 0, 0)),
            ],
        ),
        [shape((chips, rows, cols), BF16), shape((chips, rows, 128), F32)],
        block_rows * width * cols,
        2 * (block_rows * width + block_rows * cols + 2 * width * cols),
    )(side, entry, grads, w_qkv)


def exchange(value, axis, step):
    size = lax.axis_size(axis)
    return lax.ppermute(value, axis, [(i, i ^ step) for i in range(size)])


def total_over(value, axis, step=1):
    while step < lax.axis_size(axis):
        value = value + exchange(value, axis, step)
        step *= 2
    return value


@jax.tree_util.register_pytree_node_class
class Halves:
    def __init__(self, values, axes):
        self.values, self.axes = tuple(values), tuple(axes)

    def tree_flatten(self):
        return self.values, self.axes

    @classmethod
    def tree_unflatten(cls, axes, values):
        return cls(values, axes)

    def orders(self, batches):
        bits = tuple(range(1, batches.bit_length() - 1))
        return bits, bits[::-1]

    def send(self, step, batches):
        done = [send_half(v, a, o[step]) for v, a, o in zip(self.values, self.axes, self.orders(batches))]
        kept, got, axes = zip(*done)
        return Halves(kept, axes), got

    def add(self, got):
        values = [v.astype(F32) + g.astype(F32) for v, g in zip(self.values, got)]
        return Halves(values, self.axes)

    def double(self, step, batches):
        done = []
        for value, axes, order in zip(self.values, self.axes, self.orders(batches)):
            got = exchange(value, DP, 1 << order[step])
            done.append((jnp.stack([value, got]), (order[step],) + axes))
        return Halves(*zip(*done))

    def pieces(self, batches):
        bits = self.orders(batches)[1]
        done = []
        for value, axes in zip(self.values, self.axes):
            rest = list(range(len(axes), value.ndim))
            value = value.transpose([axes.index(bit) for bit in bits] + rest)
            done.append(value.reshape((batches // 2,) + value.shape[len(axes) :]))
        return jnp.concatenate(done, axis=2)


def send_half(value, axes, bit):
    own = lax.rem(lax.div(lax.axis_index(DP), 1 << bit), 2)
    at = axes.index(bit)
    sent = lax.dynamic_index_in_dim(value, 1 - own, at, False).astype(BF16)
    kept = lax.dynamic_index_in_dim(value, own, at, False)
    return kept, exchange(sent, DP, 1 << bit), axes[:at] + axes[at + 1 :]


def halves_of(first, second):
    bits = first.shape[0].bit_length() - 1
    axes = tuple(range(1, bits + 1))[::-1]
    return Halves([v.reshape((2,) * bits + v.shape[1:]) for v in (first, second)], (axes, axes))


def join(*values):
    return lax.optimization_barrier(values)


def add_low(a, b):
    return (a.astype(F32) + b.astype(F32)).astype(BF16)


class RingSum:
    def __init__(self, shift):
        self.parts, self.shift, self.step, self.moving = [], shift, 0, None

    def add(self):
        self.step += 1
        if self.step < len(self.parts):
            part = self.parts[self.step]
            self.moving = part if self.step == 1 else add_low(self.moving, part)

    def send(self):
        if self.step < len(self.parts):
            self.moving = self.shift(self.moving)

    def hop(self):
        self.add()
        self.send()


def total_of(own, got):
    total = own.astype(F32)
    for value in got:
        total = total + value.astype(F32)
    return total


def local(
    tokens,
    seq_lengths,
    attn_gain,
    mlp_gain,
    q_gain,
    k_gain,
    w_query,
    key_weight,
    value_weight,
    w_out,
    w_gate,
    w_up,
    w_down,
    out_grad,
):
    n = lax.axis_size("tensor")
    batches = lax.axis_size(DP)
    rows, width = tokens.shape
    block_rows = rows * n
    dim = q_gain.shape[0]
    heads = w_query.shape[1] // dim
    kv_heads = key_weight.shape[1] // dim
    z = lax.axis_index("tensor").astype(jnp.int32)
    zs = z.reshape(1)
    ring = [(i, (i + 1) % n) for i in range(n)]
    shift = lambda v, d=1: lax.ppermute(v, "tensor", [(i, (i + d) % n) for i in range(n)])
    shard_of = lambda s: lax.rem(z - s + n, n).reshape(1)

    chips = batches // 2
    core = lax.axis_index("core").astype(jnp.int32).reshape(1)
    place = jnp.stack([z, lax.axis_index("chip").astype(jnp.int32), core[0]])
    steps = batches.bit_length() - 2

    own_cols = width // batches
    piece = lax.dynamic_slice_in_dim(w_out, lax.axis_index(DP) * own_cols, own_cols, 1)
    piece = lax.all_gather(piece, "tensor", axis=0, tiled=False)

    offset, position = positions_of(seq_lengths[0], block_rows)
    start = offset[None, :]
    cosine, sine = rope_tables(position, dim)
    w_qkv = jnp.concatenate([w_query, key_weight, value_weight], axis=1)
    gain_one, gain_two = attn_gain[None, :], mlp_gain[None, :]
    qg, kg = q_gain[None, :], k_gain[None, :]

    came = shift(tokens)
    came, piece, w_qkv, cosine, sine, start = join(came, piece, w_qkv, cosine, sine, start)
    blocks = [tokens, came]
    middle = piece.shape[1] // 2
    halves = Halves((piece[:, :middle], piece[:, middle:]), ((), ()))
    kept, ready = None, 0
    for s in range(1, n):
        came = shift(blocks[s]) if s < n - 1 else None
        while ready <= s:
            kept = qkv_shard(
                shard_of(ready), blocks[ready], gain_one, w_qkv, cosine, sine, qg, kg, heads, kv_heads,
                dim, block_rows, kept,
            )
            ready += 1
        if s <= steps:
            halves = halves.double(s - 1, batches)
        if came is not None:
            came, kept, halves = join(came, kept, halves)
            blocks.append(came)
    entry_all, side, raw = kept
    w_own = halves.pieces(batches)
    w_other = exchange(w_own, "core", 1)

    later_grad, _ = join(out_grad, blocks[-1])
    grad_all = lax.all_gather(later_grad, "tensor", axis=0, tiled=True)

    mixed, lse = attention_forward(zs, side, start, n, heads, kv_heads, dim)
    mixed, w_own = join(mixed, w_own)
    mixed = [mixed[0]] + [shift(mixed[d], d) for d in range(1, n)]
    mixed, w_other = join(mixed, w_other)
    hidden, mlp_entry = out_projection(place, mixed, w_own, w_other, tokens, gain_two, n)

    weights = (w_gate, w_up, w_down)
    inner_sum = RingSum(shift)
    down_one, down_two, down_parts = RingSum(shift), RingSum(shift), []
    over_dp = lambda g: lax.psum_scatter(g, DP, scatter_dimension=0, tiled=False)
    blocks, kept = [mlp_entry], None
    for t in range(2 * n - 2):
        if t < n - 1:
            blocks.append(shift(blocks[t]))
        if t >= n - 1:
            inner_sum.hop()
        s = (0, -1)[t] if t < 2 else t - 1
        if 0 <= s < n:
            kept, down, inner = mlp_shard(
                shard_of(s), blocks[s], grad_all if s else out_grad, weights, kept, block_rows
            )
            down_parts.append(down)
            inner_sum.parts.append(inner)
        if s >= n:
            down_one.parts = [part[:, : width // 2] for part in down_parts]
            down_two.parts = [part[:, width // 2 :] for part in down_parts]
            down_one.hop()
            mlp_grads = rows_grad(grad_all, [active], 2, batches, None)
            mlp_grads = rows_grad(mlp_all, [gate_grad, up_grad], 0, batches, mlp_grads)
            inner_sum.moving, down_one.moving, mlp_grads = join(
                inner_sum.moving, down_one.moving, mlp_grads
            )
            mlp_grads = over_dp(mlp_grads)
        else:
            state = (blocks, kept, inner_sum.parts, inner_sum.moving)
            state, grad_all = join(state, grad_all) if t else (join(*state), grad_all)
            blocks, kept, inner_sum.parts, inner_sum.moving = state
            active, gate_grad, up_grad, mlp_all = kept

    down_two.hop()
    gm, grad_hidden, grad_mid, mlp_part = mid_stage(
        place, inner_sum.parts[0], (inner_sum.moving,), out_grad, hidden, gain_two, w_own, w_other, n
    )
    gm, grad_mid, down_two.moving = join(gm, grad_mid, down_two.moving)

    gm = [gm[0]] + [shift(gm[d], d) for d in range(1, n)]
    (got,) = out_weight_grad(place, 1 - core, mixed, grad_mid, n, chips, None)
    down_one.add()
    down_two.add()
    gm, got, down_one.moving, down_two.moving = join(gm, got, down_one.moving, down_two.moving)

    down_one.send()
    got = exchange(got, "core", 1)
    grads, gain_parts = attention_backward(
        zs, gm, side, raw, lse, start, cosine, sine, qg, kg, heads, kv_heads, dim
    )
    grads, got, down_one.moving = join(grads, got, down_one.moving)
    down_two.send()
    down_one.hop()
    entry_part = lambda s: entry_shard(shard_of(s), grads, w_qkv, rows)
    entry_sum = RingSum(shift)
    entry_sum.parts = [None, entry_part(1)] + [None] * (n - 2)
    w_out_grad = out_weight_grad(place, core, mixed, grad_mid, n, chips, got)
    entry_sum.parts[1], grads, w_out_grad, down_one.moving, down_two.moving = join(
        entry_sum.parts[1], grads, w_out_grad, down_one.moving, down_two.moving
    )

    out_one, out_two = halves_of(*w_out_grad[:2]), halves_of(*w_out_grad[2:])
    entry_sum.add()

    entry_sum.send()
    down_two.hop()
    out_one, one_got = out_one.send(0, batches)
    qkv_sent, lanes_sent = qkv_weight_grad(1 - core, entry_all, grads, w_qkv, chips)
    w_qkv_grad, lanes = qkv_weight_grad(core, entry_all, grads, w_qkv, chips)
    entry_sum.parts[2 % n] = entry_part(2 % n)
    entry_sum.add()
    state = (entry_sum.moving, down_two.moving, qkv_sent, w_qkv_grad)
    state, grads, lanes, lanes_sent, out_one, one_got, out_two = join(
        state, grads, lanes, lanes_sent, out_one, one_got, out_two
    )
    entry_sum.moving, down_two.moving, qkv_sent, w_qkv_grad = state
    lanes, lanes_sent = jnp.sum(lanes, axis=2), jnp.sum(lanes_sent, axis=2)
    lanes = jnp.where(core[0] == 0, jnp.stack([lanes, lanes_sent], 1), jnp.stack([lanes_sent, lanes], 1))
    attn_part = lanes.reshape(width) / attn_gain
    totals = jnp.concatenate([attn_part, mlp_part[0], gain_parts[0], gain_parts[1]])[None, :]

    entry_sum.send()
    out_two, two_got = out_two.send(0, batches)
    qkv_got = exchange(qkv_sent, "core", 1)
    totals = total_over(totals, DP)
    entry_sum.parts[3 % n] = entry_part(3 % n)
    entry_sum.add()
    while down_one.step < n - 1:
        down_one.hop()
        down_two.hop()
    moved = jnp.concatenate([down_one.moving, down_two.moving], axis=1)
    output = total_of(hidden, [down_parts[0], moved]).astype(BF16)
    state = (entry_sum.moving, out_one, one_got, out_two, two_got, qkv_got, w_qkv_grad)
    state, grads, totals, output = join(state, grads, totals, output)
    entry_sum.moving, out_one, one_got, out_two, two_got, qkv_got, w_qkv_grad = state

    totals = totals + exchange(totals, "tensor", 1)
    out_one, out_two = out_one.add(one_got), out_two.add(two_got)
    values = [jnp.concatenate(pair, axis=-3) for pair in zip(out_one.values, out_two.values)]
    out_halves = Halves(values, out_one.axes)
    for step in range(1, steps):
        out_halves, out_got = out_halves.send(step, batches)
        out_got, w_qkv_grad, qkv_got = join(out_got, w_qkv_grad, qkv_got)
        out_halves = out_halves.add(out_got)
    w_out_grad = jnp.concatenate(out_halves.values, axis=-1).astype(BF16)
    out_sum = RingSum(shift)
    out_sum.parts = [lax.dynamic_index_in_dim(w_out_grad, shard_of(d)[0], 0, False) for d in range(n)]
    out_sum.hop()
    units = w_gate.shape[1]
    mlp_grads = mlp_grads.astype(F32)
    mlp_grads = mlp_grads[:, :units], mlp_grads[:, units : 2 * units], mlp_grads[:, 2 * units :].T
    out_sum.moving, mlp_grads, totals = join(out_sum.moving, mlp_grads, totals)
    for _ in range(n - 2):
        out_sum.hop()
    middle = w_qkv_grad.shape[-1] // 2
    qkv_halves = halves_of(
        add_low(w_qkv_grad[..., :middle], qkv_got[..., :middle]),
        add_low(w_qkv_grad[..., middle:], qkv_got[..., middle:]),
    )
    for step in range(steps):
        qkv_halves, qkv_got = qkv_halves.send(step, batches)
        if step < steps - 1:
            qkv_halves = qkv_halves.add(qkv_got)
    totals = total_over(totals, "tensor", 2)
    for s in range(3, n):
        entry_sum.send()
        entry_sum.parts[(s + 1) % n] = entry_part((s + 1) % n)
        if s < n - 1:
            entry_sum.add()
            entry_sum.moving, grads = join(entry_sum.moving, grads)
    grad_entry = total_of(entry_sum.parts[0], [entry_sum.moving])
    w_out_grad = total_of(out_sum.parts[0], [out_sum.moving])
    w_qkv_grad = jnp.concatenate(qkv_halves.add(qkv_got).values, axis=-1)

    x = tokens.astype(F32)
    scale = inv_root_of(x)
    token_grad = (grad_hidden + norm_back(grad_entry * attn_gain, x * scale, scale)).astype(BF16)

    totals = totals[0]
    attn_gain_grad = totals[:width]
    mlp_gain_grad = totals[width : 2 * width]
    q_gain_grad = totals[2 * width : 2 * width + dim]
    k_gain_grad = totals[2 * width + dim :]
    a, b = heads * dim, (heads + kv_heads) * dim
    return (
        output,
        token_grad,
        attn_gain_grad,
        mlp_gain_grad,
        q_gain_grad,
        k_gain_grad,
        w_qkv_grad[:, :a],
        w_qkv_grad[:, a:b],
        w_qkv_grad[:, b:],
        w_out_grad,
        *mlp_grads,
    )


def solution(mesh):
    batches, shards = mesh.shape["dp"], mesh.shape["tensor"]
    return jax.shard_map(
        local,
        mesh=Mesh(mesh.devices.reshape(batches // 2, 2, shards), DP + ("tensor",)),
        in_specs=(
            P(("chip", "core", "tensor"), None),
            P(DP, None),
            P(),
            P(),
            P(),
            P(),
            P(None, "tensor"),
            P(None, "tensor"),
            P(None, "tensor"),
            P("tensor", None),
            P(None, "tensor"),
            P(None, "tensor"),
            P("tensor", None),
            P(("chip", "core", "tensor"), None),
        ),
        out_specs=(
            P(("chip", "core", "tensor"), None),
            P(("chip", "core", "tensor"), None),
            P(),
            P(),
            P(),
            P(),
            P(DP, "tensor"),
            P(DP, "tensor"),
            P(DP, "tensor"),
            P("tensor", DP),
            P(DP, "tensor"),
            P(DP, "tensor"),
            P("tensor", DP),
        ),
        check_vma=False,
    )
```
